128 devices in a mesh: frame: 16 (over z_lo, y, core), strip: 8 (over z_hi, x).
Axes of the slice: x: 4, y: 4, z: 4 (z_hi: 2, z_lo: 2; z = z_hi * 2 + z_lo), core: 2. Of those that a mesh axis runs over, the one named last changes fastest.
Arguments:
- latents: bfloat16 [32, 64, 128, 512], P('frame', None, 'strip'), may hold values from -29 to 38
- norm_first: float32 [2, 512], replicated, may hold values from -2 to 2, as said below
- conv_first: bfloat16 [3, 3, 512, 512], replicated, may hold values from -0.09375 to 0.09375
- bias_first: float32 [512], replicated, may hold values from -3 to 3
- norm_second: float32 [2, 512], replicated, may hold values from -2 to 2, as said below
- conv_second: bfloat16 [3, 3, 512, 512], replicated, may hold values from -0.09375 to 0.09375
- bias_second: float32 [512], replicated, may hold values from -3 to 3
- norm_third: float32 [2, 512], replicated, may hold values from -2 to 2, as said below
- time_first: bfloat16 [3, 512, 512], replicated, may hold values from -0.15625 to 0.15625
- tbias_first: float32 [512], replicated, may hold values from -3 to 3
- norm_fourth: float32 [2, 512], replicated, may hold values from -2 to 2, as said below
- time_second: bfloat16 [3, 512, 512], replicated, may hold values from -0.15625 to 0.15625
- tbias_second: float32 [512], replicated, may hold values from -3 to 3
- mix_factor: float32 [1], replicated, may hold values from -2 to 1
Outputs:
- mixed: bfloat16 [32, 64, 128, 512], P('frame', None, 'strip')
The draws below stay inside these ranges and needn't reach their ends.
Inputs may be any that keep to these rules, and one draw needn't show every extreme that they name: `norm_first`: row 0 holds gains, row 1 shifts. `norm_second`: row 0 holds gains, row 1 shifts. `norm_third`: row 0 holds gains, row 1 shifts. `norm_fourth`: row 0 holds gains, row 1 shifts.
All inputs are finite; a program needn't handle non-finite values.
Results may differ from the reference program's by a relative error of at most 0.013.
Values may be sent and summed in bfloat16 or wider, within the bound.
A program may use at most 128 MiB of HBM per device.

```python
import math
import jax
import jax.numpy as jnp
from jax import lax

C = 512
GROUPS = 32
ROWS = 64
WIDTH = 128
FRAMES = 32


def norm_params(key, salt):
    key = jax.random.fold_in(key, salt)
    key_gain, key_shift = jax.random.split(key)
    gains = jax.random.uniform(key_gain, (C,), jnp.float32, 0.5, 1.5)
    shifts = jnp.clip(0.5 * jax.random.normal(key_shift, (C,), jnp.float32), -2.0, 2.0)
    return jnp.stack([gains, shifts])


def draw_norm_first(key, part):
    return norm_params(key, 11)


def draw_norm_second(key, part):
    return norm_params(key, 12)


def draw_norm_third(key, part):
    return norm_params(key, 13)


def draw_norm_fourth(key, part):
    return norm_params(key, 14)


def draw_latents(key, part):
    key = jax.random.fold_in(key, 3)
    key_base = jax.random.fold_in(key, 0)
    key_chan = jax.random.fold_in(key, 1)
    key_kind = jax.random.fold_in(key, 3)
    key_shift = jax.random.fold_in(key, 4)
    key_rowf = jax.random.fold_in(key, 5)
    key_colf = jax.random.fold_in(key, 6)
    channel_scale = jnp.exp(jax.random.uniform(key_chan, (C,), jnp.float32, math.log(0.3), math.log(3.0)))
    frame_frac = jnp.arange(FRAMES, dtype=jnp.float32) / max(FRAMES - 1, 1)
    column_frac = jnp.arange(WIDTH, dtype=jnp.float32) / max(WIDTH - 1, 1)
    frame_scale = 3.0 ** frame_frac
    column_scale = 2.0 ** column_frac
    scaling = 0.15 * frame_scale[:, None, None, None] * column_scale[None, None, :, None] * channel_scale
    flat_frame = (jax.random.permutation(key_kind, FRAMES) < FRAMES // 2)[:, None, None, None]
    row_factor = jnp.exp(jax.random.uniform(key_rowf, (FRAMES, ROWS, 1, 1), jnp.float32, math.log(0.5), math.log(2.0)))
    column_factor = jnp.exp(jax.random.uniform(key_colf, (FRAMES, 1, WIDTH, 1), jnp.float32, math.log(0.5), math.log(2.0)))
    noise = jnp.clip(jax.random.normal(key_base, (FRAMES, ROWS, WIDTH, C), jnp.float32), -2.5, 2.5)
    frame_shift = jnp.clip(jax.random.normal(key_shift, (FRAMES, 1, 1, C), jnp.float32), -3.0, 3.0)
    offset = (0.5 + column_frac)[None, None, :, None] * (0.6 + 1.4 * frame_frac)[:, None, None, None]
    flat_field = 1.2 * frame_shift + 0.2 * noise
    contrast_field = noise * row_factor * column_factor + 0.3 * frame_shift
    base_values = jnp.where(flat_frame, flat_field, contrast_field) + offset
    return (base_values * scaling).astype(jnp.bfloat16)


def bell_draw(stream_key, extent, width, reach, kind=jnp.bfloat16):
    return jnp.clip(width * jax.random.normal(stream_key, extent, jnp.float32), -reach, reach).astype(kind)


def setup_inputs(seed: int = 0) -> dict:
    streams_of = jax.random.split(jax.random.key(seed), 15)
    latents = draw_latents(jax.random.fold_in(streams_of[14], 71), 0)
    norm_first = draw_norm_first(jax.random.fold_in(streams_of[14], 71), 0)
    conv_first = bell_draw(streams_of[2], (3, 3, C, C), (9 * C) ** -0.5, 0.09375)
    bias_first = bell_draw(streams_of[3], (C,), 0.5, 3.0, jnp.float32)
    norm_second = draw_norm_second(jax.random.fold_in(streams_of[14], 71), 0)
    conv_second = bell_draw(streams_of[5], (3, 3, C, C), (9 * C) ** -0.5, 0.09375)
    bias_second = bell_draw(streams_of[6], (C,), 0.5, 3.0, jnp.float32)
    norm_third = draw_norm_third(jax.random.fold_in(streams_of[14], 71), 0)
    time_first = bell_draw(streams_of[8], (3, C, C), (3 * C) ** -0.5, 0.15625)
    tbias_first = bell_draw(streams_of[9], (C,), 0.5, 3.0, jnp.float32)
    norm_fourth = draw_norm_fourth(jax.random.fold_in(streams_of[14], 71), 0)
    time_second = bell_draw(streams_of[11], (3, C, C), (3 * C) ** -0.5, 0.15625)
    tbias_second = bell_draw(streams_of[12], (C,), 0.5, 3.0, jnp.float32)
    mix_factor = jnp.clip(jax.random.uniform(streams_of[13], (1,), jnp.float32, -2.0, 1.0), -2.0, 1.0)
    return {"latents": latents, "norm_first": norm_first, "conv_first": conv_first, "bias_first": bias_first, "norm_second": norm_second, "conv_second": conv_second, "bias_second": bias_second, "norm_third": norm_third, "time_first": time_first, "tbias_first": tbias_first, "norm_fourth": norm_fourth, "time_second": time_second, "tbias_second": tbias_second, "mix_factor": mix_factor}


eps_norm = 1e-06

def group_norm_act(values, params, reduce_axes):
    widened = values.astype(jnp.float32)
    grouped = widened.reshape(widened.shape[:3] + (GROUPS, widened.shape[3] // GROUPS))
    average = lax.optimization_barrier(jnp.mean(grouped, axis=reduce_axes + (4,), keepdims=True))
    variance = lax.optimization_barrier(jnp.mean((grouped - average) ** 2, axis=reduce_axes + (4,), keepdims=True))
    normed = ((grouped - average) * lax.rsqrt(variance + eps_norm)).reshape(widened.shape)
    return jax.nn.silu(normed * params[0] + params[1]).astype(jnp.bfloat16)

def spatial_conv(activation, kernel):
    return lax.conv_general_dilated(activation.astype(jnp.float32), kernel.astype(jnp.float32), (1, 1), ((1, 1), (1, 1)), dimension_numbers=('NHWC', 'HWIO', 'NHWC'), precision=lax.Precision.HIGHEST)

def temporal_conv(activation, weight):
    frames_all = activation.shape[0]
    padded = jnp.pad(activation.astype(jnp.float32), ((1, 1), (0, 0), (0, 0), (0, 0)))
    result = jnp.zeros(activation.shape, jnp.float32)
    for offset in range(3):
        result = result + jnp.einsum('frwc,cd->frwd', padded[offset:offset + frames_all], weight[offset].astype(jnp.float32), precision=lax.Precision.HIGHEST)
    return result

def reference(latents, norm_first, conv_first, bias_first, norm_second, conv_second, bias_second, norm_third, time_first, tbias_first, norm_fourth, time_second, tbias_second, mix_factor):
    first = (spatial_conv(group_norm_act(latents, norm_first, (1, 2)), conv_first) + bias_first).astype(jnp.bfloat16)
    second = spatial_conv(group_norm_act(first, norm_second, (1, 2)), conv_second) + bias_second
    spatial = (latents.astype(jnp.float32) + second).astype(jnp.bfloat16)
    tempo = (temporal_conv(group_norm_act(spatial, norm_third, (0, 1, 2)), time_first) + tbias_first).astype(jnp.bfloat16)
    branch = temporal_conv(group_norm_act(tempo, norm_fourth, (0, 1, 2)), time_second) + tbias_second
    blend_factor = jax.nn.sigmoid(mix_factor[0])
    widened = spatial.astype(jnp.float32)
    return (blend_factor * widened + (1.0 - blend_factor) * (widened + branch)).astype(jnp.bfloat16)
```

```python
import functools

import jax
import jax.numpy as jnp
from jax import lax
from jax.experimental import pallas as pl
from jax.experimental.pallas import tpu as pltpu
from jax.sharding import PartitionSpec as P

MESH = pl.DeviceIdType.MESH
F32 = jnp.float32
BF16 = jnp.bfloat16
C = 512
ROWS = 64
COLS = 16
PAIRS = COLS // 2
POS = ROWS * COLS
GROUP = 16
HALF = 256
EPS = 1e-06


def drain(ref, sem):
    pltpu.make_async_copy(ref, ref, sem).wait()


def combine(tiles, count):
    n = tiles.shape[0]
    means, squares = tiles[:, 0:4, :], tiles[:, 4:8, :]
    mean = jnp.sum(means, axis=0) * (1.0 / n)
    gap = means - mean[None]
    return mean, jnp.sum(squares, axis=0) + count * jnp.sum(gap * gap, axis=0)


def row_of(tile):
    return jnp.concatenate([tile[q : q + 1, :] for q in range(4)], axis=1)


def coefficients(mean, square, count, group_sum, params):
    eight = jnp.concatenate([mean, mean], axis=0)
    centre = jnp.dot(eight, group_sum, preferred_element_type=F32, precision=lax.Precision.HIGHEST)
    centre = centre[0:4] * (1.0 / GROUP)
    gap = mean - centre
    total = square + count * gap * gap
    total = jnp.concatenate([total, total], axis=0)
    spread = jnp.dot(total, group_sum, preferred_element_type=F32, precision=lax.Precision.HIGHEST)
    inverse = lax.rsqrt(spread[0:4] * (1.0 / (GROUP * count)) + EPS)
    return row_of(centre), 0.5 * row_of(inverse) * params[0:1, :], 0.5 * params[1:2, :]


def act(values, coef):
    mean, scale, shift = coef
    h = (values.astype(F32) - mean) * scale + shift
    return h + h * jnp.tanh(h)


def put_moments(tile_ref, lo, mean, square):
    for q in range(mean.shape[1] // 128):
        at = lo // 128 + q
        tile_ref[at : at + 1, :] = mean[:, q * 128 : (q + 1) * 128]
        tile_ref[at + 4 : at + 5, :] = square[:, q * 128 : (q + 1) * 128]


def kernel(
    nf,
    ns,
    lat_hbm,
    norm1,
    conv1_hbm,
    bias1,
    norm2,
    conv2_hbm,
    bias2,
    norm3,
    time1_hbm,
    tbias1,
    norm4,
    time2_hbm,
    tbias2,
    mix,
    out_hbm,
    raw,
    lx,
    halo1,
    u1,
    u2,
    tw1,
    tw2,
    s,
    v,
    fx,
    halo2,
    sp,
    near,
    far,
    dd,
    a3,
    tm,
    td,
    perm,
    st_own,
    st1,
    st2,
    st3s,
    st3f,
    st4s,
    st4f,
    load_sem,
    u1_sem,
    u2_sem,
    tw_sem,
    halo_send,
    halo_recv,
    stat_send,
    stat_recv,
    frame_send,
    frame_recv,
    out_sem,
):
    f = lax.axis_index("frame")
    st = lax.axis_index("strip")
    core = lax.rem(f, 2)
    first_frame = core
    second_frame = 1 - core
    partner = f + 1 - 2 * core
    has_peer = jnp.logical_and(f > 0, f < nf - 1)
    peer = jnp.where(has_peer, f - 1 + 2 * core, partner)
    has_left, has_right = st > 0, st < ns - 1

    barrier = pltpu.get_barrier_semaphore()
    for d in range(1, ns):
        pl.semaphore_signal(barrier, inc=1, device_id={"strip": lax.rem(st + d, ns)}, device_id_type=MESH)
    for d in range(1, nf):
        pl.semaphore_signal(barrier, inc=1, device_id={"frame": lax.rem(f + d, nf)}, device_id_type=MESH)

    load = pltpu.make_async_copy(lat_hbm, raw, load_sem)
    load.start()

    def conv_loads(hbm, u, sem):
        copies = []
        for j, slot in ((0, 0), (1, 2), (2, 3)):
            for i in range(3):
                copies.append(
                    pltpu.make_async_copy(hbm.at[i, j], u.at[slot, pl.ds(i * C, C), :], sem.at[slot, i])
                )
        for copy in copies:
            copy.start()
        return copies

    u1_loads = conv_loads(conv1_hbm, u1, u1_sem)
    u2_loads = conv_loads(conv2_hbm, u2, u2_sem)
    tw_loads = []
    for n, (hbm, tw) in enumerate(((time1_hbm, tw1), (time2_hbm, tw2))):
        for k in range(3):
            tap = k + core * (2 - 2 * k)
            tw_loads.append(pltpu.make_async_copy(hbm.at[tap], tw.at[pl.ds(k * C, C), :], tw_sem.at[n, k]))
    for copy in tw_loads:
        copy.start()

    i0 = lax.broadcasted_iota(jnp.int32, (HALF, HALF), 0)
    i1 = lax.broadcasted_iota(jnp.int32, (HALF, HALF), 1)
    perm[...] = jnp.where(i1 == (i0 & 15) * 16 + (i0 >> 4), 1.0, 0.0).astype(BF16)
    g0 = lax.broadcasted_iota(jnp.int32, (128, 128), 0)
    g1 = lax.broadcasted_iota(jnp.int32, (128, 128), 1)
    group_sum = jnp.where((g0 >> 4) == (g1 >> 4), 1.0, 0.0).astype(F32)

    s[:, 0:8, :] = jnp.zeros((COLS + 2, 8, C), F32)
    s[:, 72:80, :] = jnp.zeros((COLS + 2, 8, C), F32)

    load.wait()

    @pl.loop(0, 8)
    def _(n):
        fr, b = n // 4, lax.rem(n, 4)
        block = raw[fr, pl.ds(b * HALF, HALF), :]
        moved = jnp.dot(perm[...], block, preferred_element_type=F32)
        lx[fr, :, :, pl.ds(pl.multiple_of(b * 16, 16), 16), :] = moved.reshape(PAIRS, 2, 16, C).astype(BF16)

    for fr in range(2):
        zero = jnp.zeros((8, C), F32)

        def add_up(c, total, fr=fr):
            return total + jnp.sum(lx[fr, c // 2, lax.rem(c, 2)].astype(F32).reshape(8, 8, C), axis=0)

        mean = jnp.sum(lax.fori_loop(0, COLS, add_up, zero), axis=0, keepdims=True) * (1.0 / POS)

        def add_squares(c, total, fr=fr, mean=mean):
            gap = lx[fr, c // 2, lax.rem(c, 2)].astype(F32) - mean
            return total + jnp.sum((gap * gap).reshape(8, 8, C), axis=0)

        square = jnp.sum(lax.fori_loop(0, COLS, add_squares, zero), axis=0, keepdims=True)
        put_moments(st_own.at[fr], 0, mean, square)

    def transform_weights(u):
        @pl.loop(0, 3 * C // 32)
        def _(n):
            at = pl.ds(pl.multiple_of(n * 32, 32), 32)
            outer = (u[0, at, :].astype(F32) + u[3, at, :].astype(F32)) * 0.5
            middle = u[2, at, :].astype(F32) * 0.5
            u[1, at, :] = (outer + middle).astype(BF16)
            u[2, at, :] = (outer - middle).astype(BF16)

    for copy in u1_loads:
        copy.wait()
    transform_weights(u1)

    pl.semaphore_wait(barrier, ns - 1 + nf - 1)

    def strip_gather(src, slots, k):
        for d in range(1, ns):
            pltpu.make_async_remote_copy(
                src, slots.at[d - 1], stat_send.at[k], stat_recv.at[k],
                device_id={"strip": lax.rem(st + d, ns)}, device_id_type=MESH,
            ).start()

    def frame_gather(src, slots, k):
        for d in range(1, nf):
            pltpu.make_async_remote_copy(
                src, slots.at[d - 1], stat_send.at[k], stat_recv.at[k],
                device_id={"frame": lax.rem(f + d, nf)}, device_id_type=MESH,
            ).start()

    def gather_wait(slots, k):
        drain(slots, stat_recv.at[k])
        drain(slots, stat_send.at[k])

    def edge_copies(x, halo, fr, order, k):
        to_left = pltpu.make_async_remote_copy(
            x.at[fr, 0, 0], halo.at[order, 1], halo_send.at[k, 0], halo_recv.at[k, 1],
            device_id={"strip": lax.max(st - 1, 0)}, device_id_type=MESH,
        )
        to_right = pltpu.make_async_remote_copy(
            x.at[fr, PAIRS - 1, 1], halo.at[order, 0], halo_send.at[k, 1], halo_recv.at[k, 0],
            device_id={"strip": lax.min(st + 1, ns - 1)}, device_id_type=MESH,
        )
        return to_left, to_right

    def edges_start(x, halo, fr, order, k):
        to_left, to_right = edge_copies(x, halo, fr, order, k)
        pl.when(has_left)(lambda: to_left.start())
        pl.when(has_right)(lambda: to_right.start())

    def edges_wait(x, halo, fr, order, k):
        to_left, to_right = edge_copies(x, halo, fr, order, k)

        @pl.when(has_left)
        def _():
            to_left.wait_send()
            to_right.wait_recv()

        @pl.when(has_right)
        def _():
            to_right.wait_send()
            to_left.wait_recv()

        @pl.when(jnp.logical_not(has_left))
        def _():
            halo[order, 0] = jnp.zeros((ROWS, C), BF16)

        @pl.when(jnp.logical_not(has_right))
        def _():
            halo[order, 1] = jnp.zeros((ROWS, C), BF16)

    for order, fr in ((0, first_frame), (1, second_frame)):
        edges_start(lx, halo1, fr, order, order)
    strip_gather(st_own.at[pl.ds(0, 2)], st1, 0)

    for copy in u2_loads:
        copy.wait()
    transform_weights(u2)

    gather_wait(st1, 0)

    def spatial_stage(x, halo, fr, order, coef, u, finish):
        @pl.loop(0, COLS)
        def _(c):
            s[c + 1, 8:72, :] = act(x[fr, c // 2, lax.rem(c, 2)], coef)

        s[0, 8:72, :] = jnp.where(has_left, act(halo[order, 0], coef), 0.0)
        s[COLS + 1, 8:72, :] = jnp.where(has_right, act(halo[order, 1], coef), 0.0)

        @pl.loop(0, PAIRS)
        def _(p):
            rows = pl.ds(pl.multiple_of(p * ROWS, ROWS), ROWS)
            for i in range(3):
                for q in range(4):
                    lanes = slice(q * 128, (q + 1) * 128)
                    d = [s[2 * p + k, 7 + i : 71 + i, lanes] for k in range(4)]
                    to = slice(i * C + q * 128, i * C + (q + 1) * 128)
                    v[0, rows, to] = (d[0] - d[2]).astype(BF16)
                    v[1, rows, to] = (d[1] + d[2]).astype(BF16)
                    v[2, rows, to] = (d[2] - d[1]).astype(BF16)
                    v[3, rows, to] = (d[1] - d[3]).astype(BF16)

        for n in range(2):
            lanes = slice(n * HALF, (n + 1) * HALF)
            m = [
                jnp.concatenate(
                    [jnp.dot(v[t, h * HALF : (h + 1) * HALF], u[t, :, lanes], preferred_element_type=F32) for h in range(2)],
                    axis=0,
                )
                for t in range(4)
            ]
            finish(n, lanes, m[0] + m[1] + m[2], m[1] - m[2] - m[3])

    def moments_of(parts):
        count = sum(part.shape[0] for part in parts)
        mean = sum(jnp.sum(part, axis=0, keepdims=True) for part in parts) * (1.0 / count)
        square = sum(jnp.sum((part - mean) * (part - mean), axis=0, keepdims=True) for part in parts)
        return mean, square

    for order, fr in ((0, first_frame), (1, second_frame)):
        tiles = jnp.concatenate([st1[:, fr], st_own[fr][None]], axis=0)
        mean, square = combine(tiles, float(POS))
        coef = coefficients(mean, square, float(POS * ns), group_sum, norm1)
        edges_wait(lx, halo1, fr, order, order)

        def finish(n, lanes, even, odd, fr=fr, order=order):
            even, odd = even + bias1[:, lanes], odd + bias1[:, lanes]
            fx[fr, :, 0, :, lanes] = even.reshape(PAIRS, ROWS, HALF).astype(BF16)
            fx[fr, :, 1, :, lanes] = odd.reshape(PAIRS, ROWS, HALF).astype(BF16)
            put_moments(st_own.at[2 + order], n * HALF, *moments_of([even, odd]))

        spatial_stage(lx, halo1, fr, order, coef, u1, finish)
        edges_start(fx, halo2, fr, order, 2 + order)
        strip_gather(st_own.at[2 + order], st2.at[order], 1 + order)

    def to_peer(order, n, lanes):
        dst = near if order == 0 else far
        fr = first_frame if order == 0 else second_frame
        return pltpu.make_async_remote_copy(
            sp.at[fr, :, :, :, lanes], dst.at[:, :, :, lanes], frame_send.at[order, n], frame_recv.at[order, n],
            device_id={"frame": peer}, device_id_type=MESH,
        )

    def to_partner(n, lanes):
        return pltpu.make_async_remote_copy(
            sp.at[second_frame, :, :, :, lanes], dd.at[:, :, :, lanes], frame_send.at[2, n], frame_recv.at[2, n],
            device_id={"frame": partner}, device_id_type=MESH,
        )

    for order, fr in ((0, first_frame), (1, second_frame)):
        gather_wait(st2.at[order], 1 + order)
        tiles = jnp.concatenate([st2[order], st_own[2 + order][None]], axis=0)
        mean, square = combine(tiles, float(POS))
        coef = coefficients(mean, square, float(POS * ns), group_sum, norm2)
        edges_wait(fx, halo2, fr, order, 2 + order)

        def finish(n, lanes, even, odd, fr=fr, order=order):
            parts = []
            for k, part in enumerate((even, odd)):
                old = lx[fr, :, k, :, lanes].astype(F32).reshape(PAIRS * ROWS, HALF)
                part = (part + bias2[:, lanes]) + old
                sp[fr, :, k, :, lanes] = part.reshape(PAIRS, ROWS, HALF).astype(BF16)
                parts.append(part)
            put_moments(st_own.at[4 + order], n * HALF, *moments_of(parts))
            pl.when(has_peer)(lambda: to_peer(order, n, lanes).start())
            if order == 1:
                to_partner(n, lanes).start()

        spatial_stage(fx, halo2, fr, order, coef, u2, finish)

    def span_first(lo, slot, k, slots):
        mean, square = combine(st_own[lo : lo + 2], float(POS))
        st_own[slot] = jnp.concatenate([mean, square], axis=0)
        strip_gather(st_own.at[slot], slots, k)

    def span_second(slot, k, slots, out_slot, out_k, out_slots):
        gather_wait(slots, k)
        mean, square = combine(jnp.concatenate([slots[...], st_own[slot][None]], axis=0), float(2 * POS))
        st_own[out_slot] = jnp.concatenate([mean, square], axis=0)
        frame_gather(st_own.at[out_slot], out_slots, out_k)

    def span_done(slot, k, slots, params):
        gather_wait(slots, k)
        mean, square = combine(jnp.concatenate([slots[...], st_own[slot][None]], axis=0), float(2 * POS * ns))
        return coefficients(mean, square, float(2 * POS * ns * nf), group_sum, params)

    span_first(4, 6, 3, st3s)
    span_second(6, 3, st3s, 7, 4, st3f)
    coef3 = span_done(7, 4, st3f, norm3)

    def fill(dst, src, coef):
        @pl.loop(0, COLS)
        def _(c):
            dst[pl.ds(pl.multiple_of(c * ROWS, ROWS), ROWS), :] = act(src[c // 2, lax.rem(c, 2)], coef).astype(BF16)

    fill(a3.at[2], sp.at[first_frame], coef3)
    fill(a3.at[3], sp.at[second_frame], coef3)
    for copy in tw_loads:
        copy.wait()

    def temporal(at, tw, lanes):
        taps = jnp.concatenate([a3[at - 1], a3[at], a3[at + 1]], axis=1)
        return jnp.dot(taps, tw[:, lanes], preferred_element_type=F32)

    for n in range(2):
        lanes = slice(n * HALF, (n + 1) * HALF)
        copy = to_partner(n, lanes)
        copy.wait_send()
        copy.wait_recv()
    fill(a3.at[4], dd, coef3)

    def tempo_frame(order, moments):
        for n in range(2):
            lanes = slice(n * HALF, (n + 1) * HALF)
            values = temporal(1 + order, tw1, lanes) + tbias1[:, lanes]
            tm[order, :, :, :, lanes] = values.reshape(PAIRS, 2, ROWS, HALF).astype(BF16)
            if moments:
                put_moments(st_own.at[7 + order], n * HALF, *moments_of([values]))

    tempo_frame(2, True)
    tempo_copy = pltpu.make_async_remote_copy(
        tm.at[2], td, frame_send.at[3, 0], frame_recv.at[3, 0], device_id={"frame": partner}, device_id_type=MESH
    )
    tempo_copy.start()

    def peer_wait(order):
        @pl.when(has_peer)
        def _():
            for n in range(2):
                copy = to_peer(order, n, slice(n * HALF, (n + 1) * HALF))
                copy.wait_send()
                copy.wait_recv()

    def fill_or_zero(dst, src, coef):
        pl.when(has_peer)(lambda: fill(dst, src, coef))

        @pl.when(jnp.logical_not(has_peer))
        def _():
            @pl.loop(0, COLS)
            def _(c):
                dst[pl.ds(pl.multiple_of(c * ROWS, ROWS), ROWS), :] = jnp.zeros((ROWS, C), BF16)

    peer_wait(0)
    fill_or_zero(a3.at[1], near, coef3)
    tempo_frame(1, True)
    span_first(8, 10, 5, st4s)
    span_second(10, 5, st4s, 11, 6, st4f)

    peer_wait(1)
    fill_or_zero(a3.at[0], far, coef3)
    tempo_frame(0, False)

    coef4 = span_done(11, 6, st4f, norm4)
    fill(a3.at[2], tm.at[1], coef4)
    fill(a3.at[3], tm.at[2], coef4)
    fill_or_zero(a3.at[1], tm.at[0], coef4)
    tempo_copy.wait_send()
    tempo_copy.wait_recv()
    fill(a3.at[4], td, coef4)

    keep = 1.0 - 1.0 / (1.0 + jnp.exp(-jnp.full((1, HALF), mix[0], F32)))
    out_copies = []
    for order, fr in ((0, first_frame), (1, second_frame)):
        for n in range(2):
            lanes = slice(n * HALF, (n + 1) * HALF)
            branch = temporal(2 + order, tw2, lanes) + tbias2[:, lanes]
            old = sp[fr, :, :, :, lanes].astype(F32).reshape(POS, HALF)
            lx[fr, :, :, :, lanes] = (old + keep * branch).reshape(PAIRS, 2, ROWS, HALF).astype(BF16)

        @pl.loop(0, 4)
        def _(b, fr=fr):
            block = lx[fr, :, :, pl.ds(pl.multiple_of(b * 16, 16), 16), :].reshape(HALF, C)
            moved = jnp.dot(perm[...], block, preferred_element_type=F32)
            raw[fr, pl.ds(pl.multiple_of(b * HALF, HALF), HALF), :] = moved.astype(BF16)

        copy = pltpu.make_async_copy(raw.at[fr], out_hbm.at[fr], out_sem.at[order])
        copy.start()
        out_copies.append(copy)
    for copy in out_copies:
        copy.wait()


def body(*args):
    nf, ns = lax.axis_size("frame"), lax.axis_size("strip")
    (
        latents, norm1, conv1, bias1, norm2, conv2, bias2, norm3, time1, tbias1, norm4, time2, tbias2, mix,
    ) = args
    vmem = pl.BlockSpec(memory_space=pltpu.VMEM)
    hbm = pl.BlockSpec(memory_space=pl.ANY)
    smem = pl.BlockSpec(memory_space=pltpu.SMEM)
    tile = (8, 128)
    frame = (PAIRS, 2, ROWS, C)
    out = pl.pallas_call(
        functools.partial(kernel, nf, ns),
        out_shape=jax.ShapeDtypeStruct((2, POS, C), BF16),
        in_specs=[hbm, vmem, hbm, vmem, vmem, hbm, vmem, vmem, hbm, vmem, vmem, hbm, vmem, smem],
        out_specs=hbm,
        scratch_shapes=[
            pltpu.VMEM((2, POS, C), BF16),
            pltpu.VMEM((2,) + frame, BF16),
            pltpu.VMEM((2, 2, ROWS, C), BF16),
            pltpu.VMEM((4, 3 * C, C), BF16),
            pltpu.VMEM((4, 3 * C, C), BF16),
            pltpu.VMEM((3 * C, C), BF16),
            pltpu.VMEM((3 * C, C), BF16),
            pltpu.VMEM((COLS + 2, 80, C), F32),
            pltpu.VMEM((4, PAIRS * ROWS, 3 * C), BF16),
            pltpu.VMEM((2,) + frame, BF16),
            pltpu.VMEM((2, 2, ROWS, C), BF16),
            pltpu.VMEM((2,) + frame, BF16),
            pltpu.VMEM(frame, BF16),
            pltpu.VMEM(frame, BF16),
            pltpu.VMEM(frame, BF16),
            pltpu.VMEM((5, POS, C), BF16),
            pltpu.VMEM((3,) + frame, BF16),
            pltpu.VMEM(frame, BF16),
            pltpu.VMEM((HALF, HALF), BF16),
            pltpu.VMEM((12,) + tile, F32),
            pltpu.VMEM((ns - 1, 2) + tile, F32),
            pltpu.VMEM((2, ns - 1) + tile, F32),
            pltpu.VMEM((ns - 1,) + tile, F32),
            pltpu.VMEM((nf - 1,) + tile, F32),
            pltpu.VMEM((ns - 1,) + tile, F32),
            pltpu.VMEM((nf - 1,) + tile, F32),
            pltpu.SemaphoreType.DMA,
            pltpu.SemaphoreType.DMA((4, 3)),
            pltpu.SemaphoreType.DMA((4, 3)),
            pltpu.SemaphoreType.DMA((2, 3)),
            pltpu.SemaphoreType.DMA((4, 2)),
            pltpu.SemaphoreType.DMA((4, 2)),
            pltpu.SemaphoreType.DMA((7,)),
            pltpu.SemaphoreType.DMA((7,)),
            pltpu.SemaphoreType.DMA((4, 2)),
            pltpu.SemaphoreType.DMA((4, 2)),
            pltpu.SemaphoreType.DMA((2,)),
        ],
        compiler_params=pltpu.CompilerParams(
            collective_id=0, has_side_effects=True, vmem_limit_bytes=62 * 2**20
        ),
        cost_estimate=pl.CostEstimate(flops=20 * 10**9, bytes_accessed=17 * 2**20, transcendentals=8 * 10**6),
    )(
        latents.reshape(2, POS, C),
        norm1,
        conv1,
        bias1.reshape(1, C),
        norm2,
        conv2,
        bias2.reshape(1, C),
        norm3,
        time1,
        tbias1.reshape(1, C),
        norm4,
        time2,
        tbias2.reshape(1, C),
        mix,
    )
    return out.reshape(2, ROWS, COLS, C)


def solution(mesh):
    placed = (P("frame", None, "strip", None),) + (P(),) * 13
    return jax.shard_map(
        body, mesh=mesh, in_specs=placed, out_specs=P("frame", None, "strip", None), check_vma=False
    )
```

```python
import functools

import jax
import jax.numpy as jnp
from jax import lax
from jax.experimental import pallas as pl
from jax.experimental.pallas import tpu as pltpu
from jax.sharding import PartitionSpec as P

MESH = pl.DeviceIdType.MESH
F32 = jnp.float32
BF16 = jnp.bfloat16
C = 512
ROWS = 64
COLS = 16
PAIRS = COLS // 2
POS = ROWS * COLS
GROUP = 16
HALF = 256
EPS = 1e-06


def drain(ref, sem):
    pltpu.make_async_copy(ref, ref, sem).wait()


def combine(tiles, count):
    n = tiles.shape[0]
    means, squares = tiles[:, 0:4, :], tiles[:, 4:8, :]
    mean = jnp.sum(means, axis=0) * (1.0 / n)
    gap = means - mean[None]
    return mean, jnp.sum(squares, axis=0) + count * jnp.sum(gap * gap, axis=0)


def row_of(tile):
    return jnp.concatenate([tile[q : q + 1, :] for q in range(4)], axis=1)


def coefficients(mean, square, count, group_sum, params):
    eight = jnp.concatenate([mean, mean], axis=0)
    centre = jnp.dot(eight, group_sum, preferred_element_type=F32, precision=lax.Precision.HIGHEST)
    centre = centre[0:4] * (1.0 / GROUP)
    gap = mean - centre
    total = square + count * gap * gap
    total = jnp.concatenate([total, total], axis=0)
    spread = jnp.dot(total, group_sum, preferred_element_type=F32, precision=lax.Precision.HIGHEST)
    inverse = lax.rsqrt(spread[0:4] * (1.0 / (GROUP * count)) + EPS)
    return row_of(centre), 0.5 * row_of(inverse) * params[0:1, :], 0.5 * params[1:2, :]


def act(values, coef):
    mean, scale, shift = coef
    h = (values.astype(F32) - mean) * scale + shift
    return h + h * jnp.tanh(h)


def put_moments(tile_ref, lo, mean, square):
    for q in range(mean.shape[1] // 128):
        at = lo // 128 + q
        tile_ref[at : at + 1, :] = mean[:, q * 128 : (q + 1) * 128]
        tile_ref[at + 4 : at + 5, :] = square[:, q * 128 : (q + 1) * 128]


def kernel(
    nf,
    ns,
    lat_hbm,
    norm1,
    conv1_hbm,
    bias1,
    norm2,
    conv2_hbm,
    bias2,
    norm3,
    time1_hbm,
    tbias1,
    norm4,
    time2_hbm,
    tbias2,
    mix,
    out_hbm,
    raw,
    lx,
    halo1,
    u1,
    u2,
    tw1,
    tw2,
    s,
    v,
    fx,
    halo2,
    sp,
    near,
    far,
    dd,
    a3,
    tm,
    td,
    perm,
    st_own,
    st1,
    st2,
    st3s,
    st3f,
    st4s,
    st4f,
    load_sem,
    u1_sem,
    u2_sem,
    tw_sem,
    halo_send,
    halo_recv,
    stat_send,
    stat_recv,
    frame_send,
    frame_recv,
    out_sem,
):
    f = lax.axis_index("frame")
    st = lax.axis_index("strip")
    core = lax.rem(f, 2)
    first_frame = core
    second_frame = 1 - core
    partner = f + 1 - 2 * core
    has_peer = jnp.logical_and(f > 0, f < nf - 1)
    peer = jnp.where(has_peer, f - 1 + 2 * core, partner)
    has_left, has_right = st > 0, st < ns - 1

    barrier = pltpu.get_barrier_semaphore()
    for d in range(1, ns):
        pl.semaphore_signal(barrier, inc=1, device_id={"strip": lax.rem(st + d, ns)}, device_id_type=MESH)
    for d in range(1, nf):
        pl.semaphore_signal(barrier, inc=1, device_id={"frame": lax.rem(f + d, nf)}, device_id_type=MESH)

    load = pltpu.make_async_copy(lat_hbm, raw, load_sem)
    load.start()

    def conv_loads(hbm, u, sem):
        copies = []
        for j, slot in ((0, 0), (1, 2), (2, 3)):
            for i in range(3):
                copies.append(
                    pltpu.make_async_copy(hbm.at[i, j], u.at[slot, pl.ds(i * C, C), :], sem.at[slot, i])
                )
        for copy in copies:
            copy.start()
        return copies

    u1_loads = conv_loads(conv1_hbm, u1, u1_sem)
    u2_loads = conv_loads(conv2_hbm, u2, u2_sem)
    tw_loads = []
    for n, (hbm, tw) in enumerate(((time1_hbm, tw1), (time2_hbm, tw2))):
        for k in range(3):
            tap = k + core * (2 - 2 * k)
            tw_loads.append(pltpu.make_async_copy(hbm.at[tap], tw.at[pl.ds(k * C, C), :], tw_sem.at[n, k]))
    for copy in tw_loads:
        copy.start()

    perm[...] = transposition()
    g0 = lax.broadcasted_iota(jnp.int32, (128, 128), 0)
    g1 = lax.broadcasted_iota(jnp.int32, (128, 128), 1)
    group_sum = jnp.where((g0 >> 4) == (g1 >> 4), 1.0, 0.0).astype(F32)

    load.wait()

    for n in range(8):
        fr, b = n // 4, n % 4
        block = raw[fr, b * HALF : (b + 1) * HALF, :]
        moved = jnp.dot(perm[...], block, preferred_element_type=F32)
        lx[fr, :, :, b * 16 : (b + 1) * 16, :] = moved.reshape(PAIRS, 2, 16, C).astype(BF16)

    for fr in range(2):
        zero = jnp.zeros((8, C), F32)

        def add_up(c, total, fr=fr):
            return total + jnp.sum(lx[fr, c // 2, lax.rem(c, 2)].astype(F32).reshape(8, 8, C), axis=0)

        mean = jnp.sum(lax.fori_loop(0, COLS, add_up, zero), axis=0, keepdims=True) * (1.0 / POS)

        def add_squares(c, total, fr=fr, mean=mean):
            gap = lx[fr, c // 2, lax.rem(c, 2)].astype(F32) - mean
            return total + jnp.sum((gap * gap).reshape(8, 8, C), axis=0)

        square = jnp.sum(lax.fori_loop(0, COLS, add_squares, zero), axis=0, keepdims=True)
        put_moments(st_own.at[fr], 0, mean, square)

    def transform_weights(u):
        @pl.loop(0, 3 * C // 32)
        def _(n):
            at = pl.ds(pl.multiple_of(n * 32, 32), 32)
            outer = (u[0, at, :].astype(F32) + u[3, at, :].astype(F32)) * 0.5
            middle = u[2, at, :].astype(F32) * 0.5
            u[1, at, :] = (outer + middle).astype(BF16)
            u[2, at, :] = (outer - middle).astype(BF16)

    for copy in u1_loads:
        copy.wait()
    transform_weights(u1)

    pl.semaphore_wait(barrier, ns - 1 + nf - 1)

    def strip_gather(src, slots, k):
        for d in range(1, ns):
            pltpu.make_async_remote_copy(
                src, slots.at[d - 1], stat_send.at[k], stat_recv.at[k],
                device_id={"strip": lax.rem(st + d, ns)}, device_id_type=MESH,
            ).start()

    def frame_gather(src, slots, k):
        for d in range(1, nf):
            pltpu.make_async_remote_copy(
                src, slots.at[d - 1], stat_send.at[k], stat_recv.at[k],
                device_id={"frame": lax.rem(f + d, nf)}, device_id_type=MESH,
            ).start()

    def gather_wait(slots, k):
        drain(slots, stat_recv.at[k])
        drain(slots, stat_send.at[k])

    def edge_copies(x, halo, fr, order, k):
        to_left = pltpu.make_async_remote_copy(
            x.at[fr, 0, 0], halo.at[order, 1], halo_send.at[k, 0], halo_recv.at[k, 1],
            device_id={"strip": lax.max(st - 1, 0)}, device_id_type=MESH,
        )
        to_right = pltpu.make_async_remote_copy(
            x.at[fr, PAIRS - 1, 1], halo.at[order, 0], halo_send.at[k, 1], halo_recv.at[k, 0],
            device_id={"strip": lax.min(st + 1, ns - 1)}, device_id_type=MESH,
        )
        return to_left, to_right

    def edges_start(x, halo, fr, order, k):
        to_left, to_right = edge_copies(x, halo, fr, order, k)
        pl.when(has_left)(lambda: to_left.start())
        pl.when(has_right)(lambda: to_right.start())

    def edges_wait(x, halo, fr, order, k):
        to_left, to_right = edge_copies(x, halo, fr, order, k)

        @pl.when(has_left)
        def _():
            to_left.wait_send()
            to_right.wait_recv()

        @pl.when(has_right)
        def _():
            to_right.wait_send()
            to_left.wait_recv()

        @pl.when(jnp.logical_not(has_left))
        def _():
            halo[order, 0] = jnp.zeros((ROWS, C), BF16)

        @pl.when(jnp.logical_not(has_right))
        def _():
            halo[order, 1] = jnp.zeros((ROWS, C), BF16)

    strip_gather(st_own.at[pl.ds(0, 2)], st1, 0)
    edges_start(lx, halo1, first_frame, 0, 0)

    for copy in u2_loads:
        copy.wait()
    transform_weights(u2)

    gather_wait(st1, 0)

    def spatial_stage(x, halo, fr, order, coef, u, finish):
        @pl.loop(0, COLS, unroll=4)
        def _(c):
            s[c + 1] = act(x[fr, c // 2, lax.rem(c, 2)], coef)

        s[0] = jnp.where(has_left, act(halo[order, 0], coef), 0.0)
        s[COLS + 1] = jnp.where(has_right, act(halo[order, 1], coef), 0.0)

        @pl.loop(0, PAIRS)
        def _(p):
            rows = pl.ds(pl.multiple_of(p * ROWS, ROWS), ROWS)
            top = lax.broadcasted_iota(jnp.int32, (ROWS, 128), 0) == 0
            bottom = lax.broadcasted_iota(jnp.int32, (ROWS, 128), 0) == ROWS - 1
            for q in range(4):
                lo = q * 128
                d = [s[2 * p + k, :, lo : lo + 128] for k in range(4)]
                for t, part in enumerate((d[0] - d[2], d[1] + d[2], d[2] - d[1], d[1] - d[3])):
                    above = jnp.where(top, 0.0, pltpu.roll(part, 1, 0))
                    below = jnp.where(bottom, 0.0, pltpu.roll(part, ROWS - 1, 0))
                    v[t, rows, lo : lo + 128] = above.astype(BF16)
                    v[t, rows, C + lo : C + lo + 128] = part.astype(BF16)
                    v[t, rows, 2 * C + lo : 2 * C + lo + 128] = below.astype(BF16)

        for n in range(2):
            lanes = slice(n * HALF, (n + 1) * HALF)
            m = [
                jnp.concatenate(
                    [jnp.dot(v[t, h * HALF : (h + 1) * HALF], u[t, :, lanes], preferred_element_type=F32) for h in range(2)],
                    axis=0,
                )
                for t in range(4)
            ]
            finish(n, lanes, m[0] + m[1] + m[2], m[1] - m[2] - m[3])

    def moments_of(parts):
        count = sum(part.shape[0] for part in parts)
        mean = sum(jnp.sum(part, axis=0, keepdims=True) for part in parts) * (1.0 / count)
        square = sum(jnp.sum((part - mean) * (part - mean), axis=0, keepdims=True) for part in parts)
        return mean, square

    for order, fr in ((0, first_frame), (1, second_frame)):
        tiles = jnp.concatenate([st1[:, fr], st_own[fr][None]], axis=0)
        mean, square = combine(tiles, float(POS))
        coef = coefficients(mean, square, float(POS * ns), group_sum, norm1)
        edges_wait(lx, halo1, fr, order, order)
        if order == 0:
            edges_start(lx, halo1, second_frame, 1, 1)

        def finish(n, lanes, even, odd, fr=fr, order=order):
            even, odd = even + bias1[:, lanes], odd + bias1[:, lanes]
            fx[fr, :, 0, :, lanes] = even.reshape(PAIRS, ROWS, HALF).astype(BF16)
            fx[fr, :, 1, :, lanes] = odd.reshape(PAIRS, ROWS, HALF).astype(BF16)
            put_moments(st_own.at[2 + order], n * HALF, *moments_of([even, odd]))

        spatial_stage(lx, halo1, fr, order, coef, u1, finish)
        strip_gather(st_own.at[2 + order], st2.at[order], 1 + order)
        edges_start(fx, halo2, fr, order, 2 + order)

    def to_peer(order, n, lanes):
        dst = near if order == 0 else far
        fr = first_frame if order == 0 else second_frame
        return pltpu.make_async_remote_copy(
            sp.at[fr, :, :, :, lanes], dst.at[:, :, :, lanes], frame_send.at[order, n], frame_recv.at[order, n],
            device_id={"frame": peer}, device_id_type=MESH,
        )

    def to_partner(n, lanes):
        return pltpu.make_async_remote_copy(
            sp.at[second_frame, :, :, :, lanes], dd.at[:, :, :, lanes], frame_send.at[2, n], frame_recv.at[2, n],
            device_id={"frame": partner}, device_id_type=MESH,
        )

    for order, fr in ((0, first_frame), (1, second_frame)):
        gather_wait(st2.at[order], 1 + order)
        tiles = jnp.concatenate([st2[order], st_own[2 + order][None]], axis=0)
        mean, square = combine(tiles, float(POS))
        coef = coefficients(mean, square, float(POS * ns), group_sum, norm2)
        edges_wait(fx, halo2, fr, order, 2 + order)

        def finish(n, lanes, even, odd, fr=fr, order=order):
            parts = []
            for k, part in enumerate((even, odd)):
                old = lx[fr, :, k, :, lanes].astype(F32).reshape(PAIRS * ROWS, HALF)
                part = (part + bias2[:, lanes]) + old
                sp[fr, :, k, :, lanes] = part.reshape(PAIRS, ROWS, HALF).astype(BF16)
                parts.append(part)
            put_moments(st_own.at[4 + order], n * HALF, *moments_of(parts))
            if order == 0:
                pl.when(has_peer)(lambda: to_peer(0, n, lanes).start())
            if order == 1:
                to_partner(n, lanes).start()

        spatial_stage(fx, halo2, fr, order, coef, u2, finish)

    def span_first(lo, slot, k, slots):
        mean, square = combine(st_own[lo : lo + 2], float(POS))
        st_own[slot] = jnp.concatenate([mean, square], axis=0)
        strip_gather(st_own.at[slot], slots, k)

    def span_second(slot, k, slots, out_slot, out_k, out_slots):
        gather_wait(slots, k)
        mean, square = combine(jnp.concatenate([slots[...], st_own[slot][None]], axis=0), float(2 * POS))
        st_own[out_slot] = jnp.concatenate([mean, square], axis=0)
        frame_gather(st_own.at[out_slot], out_slots, out_k)

    def span_done(slot, k, slots, params):
        gather_wait(slots, k)
        mean, square = combine(jnp.concatenate([slots[...], st_own[slot][None]], axis=0), float(2 * POS * ns))
        return coefficients(mean, square, float(2 * POS * ns * nf), group_sum, params)

    span_first(4, 6, 3, st3s)
    span_second(6, 3, st3s, 7, 4, st3f)
    coef3 = span_done(7, 4, st3f, norm3)

    @pl.when(has_peer)
    def _():
        for n in range(2):
            to_peer(1, n, slice(n * HALF, (n + 1) * HALF)).start()

    def fill(dst, src, coef):
        @pl.loop(0, COLS, unroll=4)
        def _(c):
            dst[pl.ds(pl.multiple_of(c * ROWS, ROWS), ROWS), :] = act(src[c // 2, lax.rem(c, 2)], coef).astype(BF16)

    fill(a3.at[2], sp.at[first_frame], coef3)
    fill(a3.at[3], sp.at[second_frame], coef3)
    for copy in tw_loads:
        copy.wait()

    def temporal(at, tw, lanes):
        parts = []
        for h in range(POS // HALF):
            rows = slice(h * HALF, (h + 1) * HALF)
            taps = jnp.concatenate([a3[at - 1, rows], a3[at, rows], a3[at + 1, rows]], axis=1)
            parts.append(jnp.dot(taps, tw[:, lanes], preferred_element_type=F32))
        return jnp.concatenate(parts, axis=0)

    for n in range(2):
        lanes = slice(n * HALF, (n + 1) * HALF)
        copy = to_partner(n, lanes)
        copy.wait_send()
        copy.wait_recv()
    fill(a3.at[4], dd, coef3)

    def tempo_frame(order, moments):
        for n in range(2):
            lanes = slice(n * HALF, (n + 1) * HALF)
            values = temporal(1 + order, tw1, lanes) + tbias1[:, lanes]
            tm[order, :, :, :, lanes] = values.reshape(PAIRS, 2, ROWS, HALF).astype(BF16)
            if moments:
                put_moments(st_own.at[7 + order], n * HALF, *moments_of([values]))

    tempo_frame(2, True)
    tempo_copy = pltpu.make_async_remote_copy(
        tm.at[2], td, frame_send.at[3, 0], frame_recv.at[3, 0], device_id={"frame": partner}, device_id_type=MESH
    )
    tempo_copy.start()

    def peer_wait(order):
        @pl.when(has_peer)
        def _():
            for n in range(2):
                copy = to_peer(order, n, slice(n * HALF, (n + 1) * HALF))
                copy.wait_send()
                copy.wait_recv()

    def fill_or_zero(dst, src, coef):
        pl.when(has_peer)(lambda: fill(dst, src, coef))

        @pl.when(jnp.logical_not(has_peer))
        def _():
            @pl.loop(0, COLS)
            def _(c):
                dst[pl.ds(pl.multiple_of(c * ROWS, ROWS), ROWS), :] = jnp.zeros((ROWS, C), BF16)

    peer_wait(0)
    fill_or_zero(a3.at[1], near, coef3)
    tempo_frame(1, True)
    span_first(8, 10, 5, st4s)
    span_second(10, 5, st4s, 11, 6, st4f)

    peer_wait(1)
    fill_or_zero(a3.at[0], far, coef3)
    tempo_frame(0, False)

    coef4 = span_done(11, 6, st4f, norm4)
    fill(a3.at[2], tm.at[1], coef4)
    fill(a3.at[3], tm.at[2], coef4)
    fill_or_zero(a3.at[1], tm.at[0], coef4)
    tempo_copy.wait_send()
    tempo_copy.wait_recv()
    fill(a3.at[4], td, coef4)

    keep = 1.0 - 1.0 / (1.0 + jnp.exp(-jnp.full((1, HALF), mix[0], F32)))
    out_copies = []
    for order, fr in ((0, first_frame), (1, second_frame)):
        for n in range(2):
            lanes = slice(n * HALF, (n + 1) * HALF)
            branch = temporal(2 + order, tw2, lanes) + tbias2[:, lanes]
            old = sp[fr, :, :, :, lanes].astype(F32).reshape(POS, HALF)
            lx[fr, :, :, :, lanes] = (old + keep * branch).reshape(PAIRS, 2, ROWS, HALF).astype(BF16)

        copy = pltpu.make_async_copy(lx.at[fr], out_hbm.at[fr], out_sem.at[order])
        copy.start()
        out_copies.append(copy)
    for copy in out_copies:
        copy.wait()


def transposition():
    i0 = lax.broadcasted_iota(jnp.int32, (HALF, HALF), 0)
    i1 = lax.broadcasted_iota(jnp.int32, (HALF, HALF), 1)
    return jnp.where(i1 == (i0 & 15) * 16 + (i0 >> 4), 1.0, 0.0).astype(BF16)


def untransposed(x, out):
    moved = jnp.dot(transposition(), x[0].reshape(HALF, C), preferred_element_type=F32)
    out[0] = moved.astype(BF16)


def body(*args):
    nf, ns = lax.axis_size("frame"), lax.axis_size("strip")
    (
        latents, norm1, conv1, bias1, norm2, conv2, bias2, norm3, time1, tbias1, norm4, time2, tbias2, mix,
    ) = args
    vmem = pl.BlockSpec(memory_space=pltpu.VMEM)
    hbm = pl.BlockSpec(memory_space=pl.ANY)
    smem = pl.BlockSpec(memory_space=pltpu.SMEM)
    tile = (8, 128)
    frame = (PAIRS, 2, ROWS, C)
    out = pl.pallas_call(
        functools.partial(kernel, nf, ns),
        out_shape=jax.ShapeDtypeStruct((2,) + frame, BF16),
        in_specs=[hbm, vmem, hbm, vmem, vmem, hbm, vmem, vmem, hbm, vmem, vmem, hbm, vmem, smem],
        out_specs=hbm,
        scratch_shapes=[
            pltpu.VMEM((2, POS, C), BF16),
            pltpu.VMEM((2,) + frame, BF16),
            pltpu.VMEM((2, 2, ROWS, C), BF16),
            pltpu.VMEM((4, 3 * C, C), BF16),
            pltpu.VMEM((4, 3 * C, C), BF16),
            pltpu.VMEM((3 * C, C), BF16),
            pltpu.VMEM((3 * C, C), BF16),
            pltpu.VMEM((COLS + 2, ROWS, C), F32),
            pltpu.VMEM((4, PAIRS * ROWS, 3 * C), BF16),
            pltpu.VMEM((2,) + frame, BF16),
            pltpu.VMEM((2, 2, ROWS, C), BF16),
            pltpu.VMEM((2,) + frame, BF16),
            pltpu.VMEM(frame, BF16),
            pltpu.VMEM(frame, BF16),
            pltpu.VMEM(frame, BF16),
            pltpu.VMEM((5, POS, C), BF16),
            pltpu.VMEM((3,) + frame, BF16),
            pltpu.VMEM(frame, BF16),
            pltpu.VMEM((HALF, HALF), BF16),
            pltpu.VMEM((12,) + tile, F32),
            pltpu.VMEM((ns - 1, 2) + tile, F32),
            pltpu.VMEM((2, ns - 1) + tile, F32),
            pltpu.VMEM((ns - 1,) + tile, F32),
            pltpu.VMEM((nf - 1,) + tile, F32),
            pltpu.VMEM((ns - 1,) + tile, F32),
            pltpu.VMEM((nf - 1,) + tile, F32),
            pltpu.SemaphoreType.DMA,
            pltpu.SemaphoreType.DMA((4, 3)),
            pltpu.SemaphoreType.DMA((4, 3)),
            pltpu.SemaphoreType.DMA((2, 3)),
            pltpu.SemaphoreType.DMA((4, 2)),
            pltpu.SemaphoreType.DMA((4, 2)),
            pltpu.SemaphoreType.DMA((7,)),
            pltpu.SemaphoreType.DMA((7,)),
            pltpu.SemaphoreType.DMA((4, 2)),
            pltpu.SemaphoreType.DMA((4, 2)),
            pltpu.SemaphoreType.DMA((2,)),
        ],
        compiler_params=pltpu.CompilerParams(
            collective_id=0, has_side_effects=True, vmem_limit_bytes=62 * 2**20
        ),
        cost_estimate=pl.CostEstimate(flops=20 * 10**9, bytes_accessed=17 * 2**20, transcendentals=8 * 10**6),
    )(
        latents.reshape(2, POS, C),
        norm1,
        conv1,
        bias1.reshape(1, C),
        norm2,
        conv2,
        bias2.reshape(1, C),
        norm3,
        time1,
        tbias1.reshape(1, C),
        norm4,
        time2,
        tbias2.reshape(1, C),
        mix,
    )
    rows = pl.pallas_call(
        untransposed,
        grid=(8,),
        out_shape=jax.ShapeDtypeStruct((2, POS, C), BF16),
        in_specs=[pl.BlockSpec((1, PAIRS, 2, 16, C), lambda n: (n // 4, 0, 0, n % 4, 0))],
        out_specs=pl.BlockSpec((1, HALF, C), lambda n: (n // 4, n % 4, 0)),
        cost_estimate=pl.CostEstimate(flops=2**30, bytes_accessed=2**22, transcendentals=0),
    )(out)
    return rows.reshape(2, ROWS, COLS, C)


def solution(mesh):
    placed = (P("frame", None, "strip", None),) + (P(),) * 13
    return jax.shard_map(
        body, mesh=mesh, in_specs=placed, out_specs=P("frame", None, "strip", None), check_vma=False
    )
```

```python
import functools

import jax
import jax.numpy as jnp
from jax import lax
from jax.experimental import pallas as pl
from jax.experimental.pallas import tpu as pltpu
from jax.sharding import PartitionSpec as P

MESH = pl.DeviceIdType.MESH
F32 = jnp.float32
BF16 = jnp.bfloat16
C = 512
ROWS = 64
COLS = 16
PAIRS = COLS // 2
POS = ROWS * COLS
GROUP = 16
HALF = 256
EPS = 1e-06


def drain(ref, sem):
    pltpu.make_async_copy(ref, ref, sem).wait()


def combine(tiles, count):
    n = tiles.shape[0]
    means, squares = tiles[:, 0:4, :], tiles[:, 4:8, :]
    mean = jnp.sum(means, axis=0) * (1.0 / n)
    gap = means - mean[None]
    return mean, jnp.sum(squares, axis=0) + count * jnp.sum(gap * gap, axis=0)


def row_of(tile):
    return jnp.concatenate([tile[q : q + 1, :] for q in range(4)], axis=1)


def coefficients(mean, square, count, group_sum, params):
    eight = jnp.concatenate([mean, mean], axis=0)
    centre = jnp.dot(eight, group_sum, preferred_element_type=F32, precision=lax.Precision.HIGHEST)
    centre = centre[0:4] * (1.0 / GROUP)
    gap = mean - centre
    total = square + count * gap * gap
    total = jnp.concatenate([total, total], axis=0)
    spread = jnp.dot(total, group_sum, preferred_element_type=F32, precision=lax.Precision.HIGHEST)
    inverse = lax.rsqrt(spread[0:4] * (1.0 / (GROUP * count)) + EPS)
    return row_of(centre), 0.5 * row_of(inverse) * params[0:1, :], 0.5 * params[1:2, :]


def act(values, coef):
    mean, scale, shift = coef
    h = (values.astype(F32) - mean) * scale + shift
    return h + h * jnp.tanh(h)


def put_moments(tile_ref, lo, mean, square):
    for q in range(mean.shape[1] // 128):
        at = lo // 128 + q
        tile_ref[at : at + 1, :] = mean[:, q * 128 : (q + 1) * 128]
        tile_ref[at + 4 : at + 5, :] = square[:, q * 128 : (q + 1) * 128]


def kernel(
    nf,
    ns,
    lat_hbm,
    norm1,
    conv1_hbm,
    bias1,
    norm2,
    conv2_hbm,
    bias2,
    norm3,
    time1_hbm,
    tbias1,
    norm4,
    time2_hbm,
    tbias2,
    mix,
    out_hbm,
    raw,
    lx,
    halo1,
    u1,
    u2,
    tw1,
    tw2,
    s,
    v,
    fx,
    halo2,
    sp,
    near,
    far,
    dd,
    a3,
    tm,
    td,
    perm,
    st_own,
    st1,
    st2,
    st3s,
    st3f,
    st4s,
    st4f,
    load_sem,
    u1_sem,
    u2_sem,
    tw_sem,
    halo_send,
    halo_recv,
    stat_send,
    stat_recv,
    frame_send,
    frame_recv,
    out_sem,
):
    f = lax.axis_index("frame")
    st = lax.axis_index("strip")
    core = lax.rem(f, 2)
    first_frame = core
    second_frame = 1 - core
    partner = f + 1 - 2 * core
    has_peer = jnp.logical_and(f > 0, f < nf - 1)
    peer = jnp.where(has_peer, f - 1 + 2 * core, partner)
    has_left, has_right = st > 0, st < ns - 1

    barrier = pltpu.get_barrier_semaphore()
    for d in range(1, ns):
        pl.semaphore_signal(barrier, inc=1, device_id={"strip": lax.rem(st + d, ns)}, device_id_type=MESH)
    for d in range(1, nf):
        pl.semaphore_signal(barrier, inc=1, device_id={"frame": lax.rem(f + d, nf)}, device_id_type=MESH)

    load = pltpu.make_async_copy(lat_hbm, raw, load_sem)
    load.start()

    def conv_loads(hbm, u, sem):
        copies = []
        for j, slot in ((0, 0), (1, 2), (2, 3)):
            for i in range(3):
                copies.append(
                    pltpu.make_async_copy(hbm.at[i, j], u.at[slot, pl.ds(i * C, C), :], sem.at[slot, i])
                )
        for copy in copies:
            copy.start()
        return copies

    u1_loads = conv_loads(conv1_hbm, u1, u1_sem)
    u2_loads = conv_loads(conv2_hbm, u2, u2_sem)
    tw_loads = []
    for n, (hbm, tw) in enumerate(((time1_hbm, tw1), (time2_hbm, tw2))):
        for k in range(3):
            tap = k + core * (2 - 2 * k)
            tw_loads.append(pltpu.make_async_copy(hbm.at[tap], tw.at[pl.ds(k * C, C), :], tw_sem.at[n, k]))
    for copy in tw_loads:
        copy.start()

    perm[...] = transposition()
    g0 = lax.broadcasted_iota(jnp.int32, (128, 128), 0)
    g1 = lax.broadcasted_iota(jnp.int32, (128, 128), 1)
    group_sum = jnp.where((g0 >> 4) == (g1 >> 4), 1.0, 0.0).astype(F32)

    load.wait()

    for n in range(8):
        fr, b = n // 4, n % 4
        block = raw[fr, b * HALF : (b + 1) * HALF, :]
        moved = jnp.dot(perm[...], block, preferred_element_type=F32)
        lx[fr, :, :, b * 16 : (b + 1) * 16, :] = moved.reshape(PAIRS, 2, 16, C).astype(BF16)

    for fr in range(2):
        zero = jnp.zeros((8, C), F32)

        def add_up(c, total, fr=fr):
            return total + jnp.sum(lx[fr, c // 2, lax.rem(c, 2)].astype(F32).reshape(8, 8, C), axis=0)

        mean = jnp.sum(lax.fori_loop(0, COLS, add_up, zero), axis=0, keepdims=True) * (1.0 / POS)

        def add_squares(c, total, fr=fr, mean=mean):
            gap = lx[fr, c // 2, lax.rem(c, 2)].astype(F32) - mean
            return total + jnp.sum((gap * gap).reshape(8, 8, C), axis=0)

        square = jnp.sum(lax.fori_loop(0, COLS, add_squares, zero), axis=0, keepdims=True)
        put_moments(st_own.at[fr], 0, mean, square)

    def transform_weights(u):
        @pl.loop(0, 3 * C // 32)
        def _(n):
            at = pl.ds(pl.multiple_of(n * 32, 32), 32)
            outer = (u[0, at, :].astype(F32) + u[3, at, :].astype(F32)) * 0.5
            middle = u[2, at, :].astype(F32) * 0.5
            u[1, at, :] = (outer + middle).astype(BF16)
            u[2, at, :] = (outer - middle).astype(BF16)

    for copy in u1_loads:
        copy.wait()
    transform_weights(u1)

    pl.semaphore_wait(barrier, ns - 1 + nf - 1)

    def strip_gather(src, slots, k):
        for d in range(1, ns):
            pltpu.make_async_remote_copy(
                src, slots.at[d - 1], stat_send.at[k], stat_recv.at[k],
                device_id={"strip": lax.rem(st + d, ns)}, device_id_type=MESH,
            ).start()

    def frame_gather(src, slots, k):
        for d in range(1, nf):
            pltpu.make_async_remote_copy(
                src, slots.at[d - 1], stat_send.at[k], stat_recv.at[k],
                device_id={"frame": lax.rem(f + d, nf)}, device_id_type=MESH,
            ).start()

    def gather_wait(slots, k):
        drain(slots, stat_recv.at[k])
        drain(slots, stat_send.at[k])

    def edge_copies(x, halo, fr, order, k):
        to_left = pltpu.make_async_remote_copy(
            x.at[fr, 0, 0], halo.at[order, 1], halo_send.at[k, 0], halo_recv.at[k, 1],
            device_id={"strip": lax.max(st - 1, 0)}, device_id_type=MESH,
        )
        to_right = pltpu.make_async_remote_copy(
            x.at[fr, PAIRS - 1, 1], halo.at[order, 0], halo_send.at[k, 1], halo_recv.at[k, 0],
            device_id={"strip": lax.min(st + 1, ns - 1)}, device_id_type=MESH,
        )
        return to_left, to_right

    def edges_start(x, halo, fr, order, k):
        to_left, to_right = edge_copies(x, halo, fr, order, k)
        pl.when(has_left)(lambda: to_left.start())
        pl.when(has_right)(lambda: to_right.start())

    def edges_wait(x, halo, fr, order, k):
        to_left, to_right = edge_copies(x, halo, fr, order, k)

        @pl.when(has_left)
        def _():
            to_left.wait_send()
            to_right.wait_recv()

        @pl.when(has_right)
        def _():
            to_right.wait_send()
            to_left.wait_recv()

        @pl.when(jnp.logical_not(has_left))
        def _():
            halo[order, 0] = jnp.zeros((ROWS, C), BF16)

        @pl.when(jnp.logical_not(has_right))
        def _():
            halo[order, 1] = jnp.zeros((ROWS, C), BF16)

    strip_gather(st_own.at[pl.ds(0, 2)], st1, 0)
    edges_start(lx, halo1, first_frame, 0, 0)

    for copy in u2_loads:
        copy.wait()
    transform_weights(u2)

    gather_wait(st1, 0)

    def spatial_stage(x, halo, fr, order, coef, u, finish):
        def column(c):
            s[c + 1] = act(x[fr, c // 2, c % 2], coef)

        def pair(p):
            rows = slice(p * ROWS, (p + 1) * ROWS)
            top = lax.broadcasted_iota(jnp.int32, (ROWS, 128), 0) == 0
            bottom = lax.broadcasted_iota(jnp.int32, (ROWS, 128), 0) == ROWS - 1
            for q in range(4):
                lo = q * 128
                d = [s[2 * p + k, :, lo : lo + 128] for k in range(4)]
                for t, part in enumerate((d[0] - d[2], d[1] + d[2], d[2] - d[1], d[1] - d[3])):
                    above = jnp.where(top, 0.0, pltpu.roll(part, 1, 0))
                    below = jnp.where(bottom, 0.0, pltpu.roll(part, ROWS - 1, 0))
                    v[t, rows, lo : lo + 128] = above.astype(BF16)
                    v[t, rows, C + lo : C + lo + 128] = part.astype(BF16)
                    v[t, rows, 2 * C + lo : 2 * C + lo + 128] = below.astype(BF16)

        def products(h, n):
            lanes = slice(n * HALF, (n + 1) * HALF)
            rows = slice(h * HALF, (h + 1) * HALF)
            return [jnp.dot(v[t, rows], u[t, :, lanes], preferred_element_type=F32) for t in range(4)]

        s[0] = jnp.where(has_left, act(halo[order, 0], coef), 0.0)
        s[COLS + 1] = jnp.where(has_right, act(halo[order, 1], coef), 0.0)
        for c in range(10):
            column(c)
        for p in range(4):
            pair(p)
        early = [products(0, 0)]
        for c in range(10, COLS):
            column(c)
        for p in range(4, 6):
            pair(p)
        early.append(products(0, 1))
        for p in range(6, PAIRS):
            pair(p)
        for n in range(2):
            lanes = slice(n * HALF, (n + 1) * HALF)
            m = [jnp.concatenate(both, axis=0) for both in zip(early[n], products(1, n))]
            finish(n, lanes, m[0] + m[1] + m[2], m[1] - m[2] - m[3])

    def moments_of(parts):
        count = sum(part.shape[0] for part in parts)
        mean = sum(jnp.sum(part, axis=0, keepdims=True) for part in parts) * (1.0 / count)
        square = sum(jnp.sum((part - mean) * (part - mean), axis=0, keepdims=True) for part in parts)
        return mean, square

    for order, fr in ((0, first_frame), (1, second_frame)):
        tiles = jnp.concatenate([st1[:, fr], st_own[fr][None]], axis=0)
        mean, square = combine(tiles, float(POS))
        coef = coefficients(mean, square, float(POS * ns), group_sum, norm1)
        edges_wait(lx, halo1, fr, order, order)
        if order == 0:
            edges_start(lx, halo1, second_frame, 1, 1)

        def finish(n, lanes, even, odd, fr=fr, order=order):
            even, odd = even + bias1[:, lanes], odd + bias1[:, lanes]
            fx[fr, :, 0, :, lanes] = even.reshape(PAIRS, ROWS, HALF).astype(BF16)
            fx[fr, :, 1, :, lanes] = odd.reshape(PAIRS, ROWS, HALF).astype(BF16)
            put_moments(st_own.at[2 + order], n * HALF, *moments_of([even, odd]))

        spatial_stage(lx, halo1, fr, order, coef, u1, finish)
        strip_gather(st_own.at[2 + order], st2.at[order], 1 + order)
        edges_start(fx, halo2, fr, order, 2 + order)

    def to_peer(order, n, lanes):
        dst = near if order == 0 else far
        fr = first_frame if order == 0 else second_frame
        return pltpu.make_async_remote_copy(
            sp.at[fr, :, :, :, lanes], dst.at[:, :, :, lanes], frame_send.at[order, n], frame_recv.at[order, n],
            device_id={"frame": peer}, device_id_type=MESH,
        )

    def to_partner(n, lanes):
        return pltpu.make_async_remote_copy(
            sp.at[second_frame, :, :, :, lanes], dd.at[:, :, :, lanes], frame_send.at[2, n], frame_recv.at[2, n],
            device_id={"frame": partner}, device_id_type=MESH,
        )

    for order, fr in ((0, first_frame), (1, second_frame)):
        gather_wait(st2.at[order], 1 + order)
        tiles = jnp.concatenate([st2[order], st_own[2 + order][None]], axis=0)
        mean, square = combine(tiles, float(POS))
        coef = coefficients(mean, square, float(POS * ns), group_sum, norm2)
        edges_wait(fx, halo2, fr, order, 2 + order)

        def finish(n, lanes, even, odd, fr=fr, order=order):
            parts = []
            for k, part in enumerate((even, odd)):
                old = lx[fr, :, k, :, lanes].astype(F32).reshape(PAIRS * ROWS, HALF)
                part = (part + bias2[:, lanes]) + old
                sp[fr, :, k, :, lanes] = part.reshape(PAIRS, ROWS, HALF).astype(BF16)
                parts.append(part)
            put_moments(st_own.at[4 + order], n * HALF, *moments_of(parts))
            if order == 0:
                pl.when(has_peer)(lambda: to_peer(0, n, lanes).start())
            if order == 1:
                to_partner(n, lanes).start()

        spatial_stage(fx, halo2, fr, order, coef, u2, finish)

    def span_first(lo, slot, k, slots):
        mean, square = combine(st_own[lo : lo + 2], float(POS))
        st_own[slot] = jnp.concatenate([mean, square], axis=0)
        strip_gather(st_own.at[slot], slots, k)

    def span_second(slot, k, slots, out_slot, out_k, out_slots):
        gather_wait(slots, k)
        mean, square = combine(jnp.concatenate([slots[...], st_own[slot][None]], axis=0), float(2 * POS))
        st_own[out_slot] = jnp.concatenate([mean, square], axis=0)
        frame_gather(st_own.at[out_slot], out_slots, out_k)

    def span_done(slot, k, slots, params):
        gather_wait(slots, k)
        mean, square = combine(jnp.concatenate([slots[...], st_own[slot][None]], axis=0), float(2 * POS * ns))
        return coefficients(mean, square, float(2 * POS * ns * nf), group_sum, params)

    span_first(4, 6, 3, st3s)
    span_second(6, 3, st3s, 7, 4, st3f)
    coef3 = span_done(7, 4, st3f, norm3)

    @pl.when(has_peer)
    def _():
        for n in range(2):
            to_peer(1, n, slice(n * HALF, (n + 1) * HALF)).start()

    def temporal_stage(fills, coef, products, tw, finish):
        for h in range(POS // HALF):
            for slot, src, kept in fills:
                for c in range(4):
                    value = act(src[2 * h + c // 2, c % 2], coef)
                    if kept is not None:
                        value = jnp.where(kept, value, 0.0)
                    lo = h * HALF + c * ROWS
                    a3[slot, lo : lo + ROWS, :] = value.astype(BF16)
            rows = slice(h * HALF, (h + 1) * HALF)
            for at in products:
                taps = jnp.concatenate([a3[at - 1, rows], a3[at, rows], a3[at + 1, rows]], axis=1)
                for n in range(2):
                    lanes = slice(n * HALF, (n + 1) * HALF)
                    finish(at, h, n, lanes, jnp.dot(taps, tw[:, lanes], preferred_element_type=F32))

    for copy in tw_loads:
        copy.wait()
    for n in range(2):
        lanes = slice(n * HALF, (n + 1) * HALF)
        copy = to_partner(n, lanes)
        copy.wait_send()
        copy.wait_recv()

    def peer_wait(order):
        @pl.when(has_peer)
        def _():
            for n in range(2):
                copy = to_peer(order, n, slice(n * HALF, (n + 1) * HALF))
                copy.wait_send()
                copy.wait_recv()

    peer_wait(0)
    blocks = {}

    def tempo_finish(at, h, n, lanes, product):
        values = product + tbias1[:, lanes]
        tm[at - 1, 2 * h : 2 * h + 2, :, :, lanes] = values.reshape(2, 2, ROWS, HALF).astype(BF16)
        if at > 1:
            blocks.setdefault((at, n), []).append(moments_of([values]))

    temporal_stage(
        [(2, sp.at[first_frame], None), (3, sp.at[second_frame], None), (4, dd, None), (1, near, has_peer)],
        coef3, (3, 2), tw1, tempo_finish,
    )
    for (at, n), parts in blocks.items():
        mean = sum(part[0] for part in parts) * (1.0 / len(parts))
        square = sum(part[1] + float(HALF) * (part[0] - mean) * (part[0] - mean) for part in parts)
        put_moments(st_own.at[6 + at], n * HALF, mean, square)
    span_first(8, 10, 5, st4s)
    tempo_copy = pltpu.make_async_remote_copy(
        tm.at[2], td, frame_send.at[3, 0], frame_recv.at[3, 0], device_id={"frame": partner}, device_id_type=MESH
    )
    tempo_copy.start()
    span_second(10, 5, st4s, 11, 6, st4f)

    peer_wait(1)
    temporal_stage([(0, far, has_peer)], coef3, (1,), tw1, tempo_finish)
    tempo_copy.wait_send()
    tempo_copy.wait_recv()

    coef4 = span_done(11, 6, st4f, norm4)
    keep = 1.0 - 1.0 / (1.0 + jnp.exp(-jnp.full((1, HALF), mix[0], F32)))
    out_copies = []

    def branch_finish(at, h, n, lanes, product):
        fr = first_frame if at == 2 else second_frame
        old = sp[fr, 2 * h : 2 * h + 2, :, :, lanes].astype(F32).reshape(HALF, HALF)
        mixed = old + keep * (product + tbias2[:, lanes])
        lx[fr, 2 * h : 2 * h + 2, :, :, lanes] = mixed.reshape(2, 2, ROWS, HALF).astype(BF16)
        if n == 1:
            part = pl.ds(2 * h, 2)
            copy = pltpu.make_async_copy(lx.at[fr, part], out_hbm.at[fr, part], out_sem.at[at - 2, h])
            copy.start()
            out_copies.append(copy)

    temporal_stage(
        [(2, tm.at[1], None), (3, tm.at[2], None), (4, td, None), (1, tm.at[0], has_peer)],
        coef4, (3, 2), tw2, branch_finish,
    )
    for copy in out_copies:
        copy.wait()


def transposition():
    i0 = lax.broadcasted_iota(jnp.int32, (HALF, HALF), 0)
    i1 = lax.broadcasted_iota(jnp.int32, (HALF, HALF), 1)
    return jnp.where(i1 == (i0 & 15) * 16 + (i0 >> 4), 1.0, 0.0).astype(BF16)


def untransposed(x, out, taken, given, taken_sem, given_sem):
    blocks = [(fr, b) for fr in range(2) for b in range(4)]
    loads = [
        pltpu.make_async_copy(x.at[fr, :, :, pl.ds(b * 16, 16), :], taken.at[n], taken_sem.at[n])
        for n, (fr, b) in enumerate(blocks)
    ]
    stores = [
        pltpu.make_async_copy(given.at[n], out.at[fr, pl.ds(b * HALF, HALF), :], given_sem.at[n])
        for n, (fr, b) in enumerate(blocks)
    ]
    for load in loads:
        load.start()
    perm = transposition()
    for n in range(8):
        loads[n].wait()
        moved = jnp.dot(perm, taken[n].reshape(HALF, C), preferred_element_type=F32)
        given[n] = moved.astype(BF16)
        stores[n].start()
    for store in stores:
        store.wait()


def body(*args):
    nf, ns = lax.axis_size("frame"), lax.axis_size("strip")
    (
        latents, norm1, conv1, bias1, norm2, conv2, bias2, norm3, time1, tbias1, norm4, time2, tbias2, mix,
    ) = args
    vmem = pl.BlockSpec(memory_space=pltpu.VMEM)
    hbm = pl.BlockSpec(memory_space=pl.ANY)
    smem = pl.BlockSpec(memory_space=pltpu.SMEM)
    tile = (8, 128)
    frame = (PAIRS, 2, ROWS, C)
    out = pl.pallas_call(
        functools.partial(kernel, nf, ns),
        out_shape=jax.ShapeDtypeStruct((2,) + frame, BF16),
        in_specs=[hbm, vmem, hbm, vmem, vmem, hbm, vmem, vmem, hbm, vmem, vmem, hbm, vmem, smem],
        out_specs=hbm,
        scratch_shapes=[
            pltpu.VMEM((2, POS, C), BF16),
            pltpu.VMEM((2,) + frame, BF16),
            pltpu.VMEM((2, 2, ROWS, C), BF16),
            pltpu.VMEM((4, 3 * C, C), BF16),
            pltpu.VMEM((4, 3 * C, C), BF16),
            pltpu.VMEM((3 * C, C), BF16),
            pltpu.VMEM((3 * C, C), BF16),
            pltpu.VMEM((COLS + 2, ROWS, C), F32),
            pltpu.VMEM((4, PAIRS * ROWS, 3 * C), BF16),
            pltpu.VMEM((2,) + frame, BF16),
            pltpu.VMEM((2, 2, ROWS, C), BF16),
            pltpu.VMEM((2,) + frame, BF16),
            pltpu.VMEM(frame, BF16),
            pltpu.VMEM(frame, BF16),
            pltpu.VMEM(frame, BF16),
            pltpu.VMEM((5, POS, C), BF16),
            pltpu.VMEM((3,) + frame, BF16),
            pltpu.VMEM(frame, BF16),
            pltpu.VMEM((HALF, HALF), BF16),
            pltpu.VMEM((12,) + tile, F32),
            pltpu.VMEM((ns - 1, 2) + tile, F32),
            pltpu.VMEM((2, ns - 1) + tile, F32),
            pltpu.VMEM((ns - 1,) + tile, F32),
            pltpu.VMEM((nf - 1,) + tile, F32),
            pltpu.VMEM((ns - 1,) + tile, F32),
            pltpu.VMEM((nf - 1,) + tile, F32),
            pltpu.SemaphoreType.DMA,
            pltpu.SemaphoreType.DMA((4, 3)),
            pltpu.SemaphoreType.DMA((4, 3)),
            pltpu.SemaphoreType.DMA((2, 3)),
            pltpu.SemaphoreType.DMA((4, 2)),
            pltpu.SemaphoreType.DMA((4, 2)),
            pltpu.SemaphoreType.DMA((7,)),
            pltpu.SemaphoreType.DMA((7,)),
            pltpu.SemaphoreType.DMA((4, 2)),
            pltpu.SemaphoreType.DMA((4, 2)),
            pltpu.SemaphoreType.DMA((2, 4)),
        ],
        compiler_params=pltpu.CompilerParams(
            collective_id=0, has_side_effects=True, vmem_limit_bytes=62 * 2**20
        ),
        cost_estimate=pl.CostEstimate(flops=20 * 10**9, bytes_accessed=17 * 2**20, transcendentals=8 * 10**6),
    )(
        latents.reshape(2, POS, C),
        norm1,
        conv1,
        bias1.reshape(1, C),
        norm2,
        conv2,
        bias2.reshape(1, C),
        norm3,
        time1,
        tbias1.reshape(1, C),
        norm4,
        time2,
        tbias2.reshape(1, C),
        mix,
    )
    rows = pl.pallas_call(
        untransposed,
        out_shape=jax.ShapeDtypeStruct((2, POS, C), BF16),
        in_specs=[hbm],
        out_specs=hbm,
        scratch_shapes=[
            pltpu.VMEM((8, PAIRS, 2, 16, C), BF16),
            pltpu.VMEM((8, HALF, C), BF16),
            pltpu.SemaphoreType.DMA((8,)),
            pltpu.SemaphoreType.DMA((8,)),
        ],
        compiler_params=pltpu.CompilerParams(vmem_limit_bytes=16 * 2**20),
        cost_estimate=pl.CostEstimate(flops=2**30, bytes_accessed=2**22, transcendentals=0),
    )(out)
    return rows.reshape(2, ROWS, COLS, C)


def solution(mesh):
    placed = (P("frame", None, "strip", None),) + (P(),) * 13
    return jax.shard_map(
        body, mesh=mesh, in_specs=placed, out_specs=P("frame", None, "strip", None), check_vma=False
    )
```

```python
import functools

import jax
import jax.numpy as jnp
from jax import lax
from jax.experimental import pallas as pl
from jax.experimental.pallas import tpu as pltpu
from jax.sharding import PartitionSpec as P

MESH = pl.DeviceIdType.MESH
F32 = jnp.float32
BF16 = jnp.bfloat16
C = 512
ROWS = 64
COLS = 16
PAIRS = COLS // 2
POS = ROWS * COLS
GROUP = 16
HALF = 256
EPS = 1e-06


def drain(ref, sem):
    pltpu.make_async_copy(ref, ref, sem).wait()


def combine(tiles, count):
    n = tiles.shape[0]
    means, squares = tiles[:, 0:4, :], tiles[:, 4:8, :]
    mean = jnp.sum(means, axis=0) * (1.0 / n)
    gap = means - mean[None]
    return mean, jnp.sum(squares, axis=0) + count * jnp.sum(gap * gap, axis=0)


def row_of(tile):
    return jnp.concatenate([tile[q : q + 1, :] for q in range(4)], axis=1)


def coefficients(mean, square, count, group_sum, params):
    eight = jnp.concatenate([mean, mean], axis=0)
    centre = jnp.dot(eight, group_sum, preferred_element_type=F32, precision=lax.Precision.HIGHEST)
    centre = centre[0:4] * (1.0 / GROUP)
    gap = mean - centre
    total = square + count * gap * gap
    total = jnp.concatenate([total, total], axis=0)
    spread = jnp.dot(total, group_sum, preferred_element_type=F32, precision=lax.Precision.HIGHEST)
    inverse = lax.rsqrt(spread[0:4] * (1.0 / (GROUP * count)) + EPS)
    return row_of(centre), 0.5 * row_of(inverse) * params[0:1, :], 0.5 * params[1:2, :]


def act(values, coef):
    mean, scale, shift = coef
    h = (values.astype(F32) - mean) * scale + shift
    return h + h * jnp.tanh(h)


def put_moments(tile_ref, lo, mean, square):
    for q in range(mean.shape[1] // 128):
        at = lo // 128 + q
        tile_ref[at : at + 1, :] = mean[:, q * 128 : (q + 1) * 128]
        tile_ref[at + 4 : at + 5, :] = square[:, q * 128 : (q + 1) * 128]


def kernel(
    nf,
    ns,
    lat_hbm,
    norm1,
    conv1_hbm,
    bias1,
    norm2,
    conv2_hbm,
    bias2,
    norm3,
    time1_hbm,
    tbias1,
    norm4,
    time2_hbm,
    tbias2,
    mix,
    out_hbm,
    raw,
    lx,
    halo1,
    u1,
    u2,
    tw1,
    tw2,
    s,
    v,
    fx,
    halo2,
    sp,
    near,
    far,
    dd,
    a3,
    tm,
    td,
    perm,
    st_own,
    st1,
    st2,
    st3s,
    st3f,
    st4s,
    st4f,
    load_sem,
    u1_sem,
    u2_sem,
    tw_sem,
    halo_send,
    halo_recv,
    stat_send,
    stat_recv,
    frame_send,
    frame_recv,
    out_sem,
):
    f = lax.axis_index("frame")
    st = lax.axis_index("strip")
    core = lax.rem(f, 2)
    first_frame = core
    second_frame = 1 - core
    partner = f + 1 - 2 * core
    has_peer = jnp.logical_and(f > 0, f < nf - 1)
    peer = jnp.where(has_peer, f - 1 + 2 * core, partner)
    has_left, has_right = st > 0, st < ns - 1

    barrier = pltpu.get_barrier_semaphore()
    for d in range(1, ns):
        pl.semaphore_signal(barrier, inc=1, device_id={"strip": lax.rem(st + d, ns)}, device_id_type=MESH)
    for d in range(1, nf):
        pl.semaphore_signal(barrier, inc=1, device_id={"frame": lax.rem(f + d, nf)}, device_id_type=MESH)

    load = pltpu.make_async_copy(lat_hbm, raw, load_sem)
    load.start()

    def conv_loads(hbm, u, sem):
        copies = []
        for j, slot in ((0, 0), (1, 2), (2, 3)):
            for i in range(3):
                copies.append(
                    pltpu.make_async_copy(hbm.at[i, j], u.at[slot, pl.ds(i * C, C), :], sem.at[slot, i])
                )
        for copy in copies:
            copy.start()
        return copies

    u1_loads = conv_loads(conv1_hbm, u1, u1_sem)
    u2_loads = conv_loads(conv2_hbm, u2, u2_sem)
    tw_loads = []
    for n, (hbm, tw) in enumerate(((time1_hbm, tw1), (time2_hbm, tw2))):
        for k in range(3):
            tap = k + core * (2 - 2 * k)
            tw_loads.append(pltpu.make_async_copy(hbm.at[tap], tw.at[pl.ds(k * C, C), :], tw_sem.at[n, k]))
    for copy in tw_loads:
        copy.start()

    perm[...] = transposition()
    g0 = lax.broadcasted_iota(jnp.int32, (128, 128), 0)
    g1 = lax.broadcasted_iota(jnp.int32, (128, 128), 1)
    group_sum = jnp.where((g0 >> 4) == (g1 >> 4), 1.0, 0.0).astype(F32)

    load.wait()

    for n in range(8):
        fr, b = n // 4, n % 4
        block = raw[fr, b * HALF : (b + 1) * HALF, :]
        moved = jnp.dot(perm[...], block, preferred_element_type=F32)
        lx[fr, :, :, b * 16 : (b + 1) * 16, :] = moved.reshape(PAIRS, 2, 16, C).astype(BF16)

    for fr in range(2):
        zero = jnp.zeros((8, C), F32)

        def add_up(c, total, fr=fr):
            return total + jnp.sum(lx[fr, c // 2, lax.rem(c, 2)].astype(F32).reshape(8, 8, C), axis=0)

        mean = jnp.sum(lax.fori_loop(0, COLS, add_up, zero), axis=0, keepdims=True) * (1.0 / POS)

        def add_squares(c, total, fr=fr, mean=mean):
            gap = lx[fr, c // 2, lax.rem(c, 2)].astype(F32) - mean
            return total + jnp.sum((gap * gap).reshape(8, 8, C), axis=0)

        square = jnp.sum(lax.fori_loop(0, COLS, add_squares, zero), axis=0, keepdims=True)
        put_moments(st_own.at[fr], 0, mean, square)

    def transform_weights(u):
        @pl.loop(0, 3 * C // 32)
        def _(n):
            at = pl.ds(pl.multiple_of(n * 32, 32), 32)
            outer = (u[0, at, :].astype(F32) + u[3, at, :].astype(F32)) * 0.5
            middle = u[2, at, :].astype(F32) * 0.5
            u[1, at, :] = (outer + middle).astype(BF16)
            u[2, at, :] = (outer - middle).astype(BF16)

    for copy in u1_loads:
        copy.wait()
    transform_weights(u1)

    pl.semaphore_wait(barrier, ns - 1 + nf - 1)

    def strip_gather(src, slots, k):
        for d in range(1, ns):
            pltpu.make_async_remote_copy(
                src, slots.at[d - 1], stat_send.at[k], stat_recv.at[k],
                device_id={"strip": lax.rem(st + d, ns)}, device_id_type=MESH,
            ).start()

    def frame_gather(src, slots, k):
        for d in range(1, nf):
            pltpu.make_async_remote_copy(
                src, slots.at[d - 1], stat_send.at[k], stat_recv.at[k],
                device_id={"frame": lax.rem(f + d, nf)}, device_id_type=MESH,
            ).start()

    def gather_wait(slots, k):
        drain(slots, stat_recv.at[k])
        drain(slots, stat_send.at[k])

    def edge_copies(x, halo, fr, order, k):
        to_left = pltpu.make_async_remote_copy(
            x.at[fr, 0, 0], halo.at[order, 1], halo_send.at[k, 0], halo_recv.at[k, 1],
            device_id={"strip": lax.max(st - 1, 0)}, device_id_type=MESH,
        )
        to_right = pltpu.make_async_remote_copy(
            x.at[fr, PAIRS - 1, 1], halo.at[order, 0], halo_send.at[k, 1], halo_recv.at[k, 0],
            device_id={"strip": lax.min(st + 1, ns - 1)}, device_id_type=MESH,
        )
        return to_left, to_right

    def edges_start(x, halo, fr, order, k):
        to_left, to_right = edge_copies(x, halo, fr, order, k)
        pl.when(has_left)(lambda: to_left.start())
        pl.when(has_right)(lambda: to_right.start())

    def edges_wait(x, halo, fr, order, k):
        to_left, to_right = edge_copies(x, halo, fr, order, k)

        @pl.when(has_left)
        def _():
            to_left.wait_send()
            to_right.wait_recv()

        @pl.when(has_right)
        def _():
            to_right.wait_send()
            to_left.wait_recv()

        @pl.when(jnp.logical_not(has_left))
        def _():
            halo[order, 0] = jnp.zeros((ROWS, C), BF16)

        @pl.when(jnp.logical_not(has_right))
        def _():
            halo[order, 1] = jnp.zeros((ROWS, C), BF16)

    strip_gather(st_own.at[pl.ds(0, 2)], st1, 0)
    edges_start(lx, halo1, first_frame, 0, 0)

    for copy in u2_loads:
        copy.wait()
    transform_weights(u2)

    gather_wait(st1, 0)

    def spatial_stage(x, halo, fr, order, coef, u, finish):
        def column(c):
            s[c + 1] = act(x[fr, c // 2, c % 2], coef)

        def pair(p):
            rows = slice(p * ROWS, (p + 1) * ROWS)
            top = lax.broadcasted_iota(jnp.int32, (ROWS, 128), 0) == 0
            bottom = lax.broadcasted_iota(jnp.int32, (ROWS, 128), 0) == ROWS - 1
            for q in range(4):
                lo = q * 128
                d = [s[2 * p + k, :, lo : lo + 128] for k in range(4)]
                for t, part in enumerate((d[0] - d[2], d[1] + d[2], d[2] - d[1], d[1] - d[3])):
                    above = jnp.where(top, 0.0, pltpu.roll(part, 1, 0))
                    below = jnp.where(bottom, 0.0, pltpu.roll(part, ROWS - 1, 0))
                    v[t, rows, lo : lo + 128] = above.astype(BF16)
                    v[t, rows, C + lo : C + lo + 128] = part.astype(BF16)
                    v[t, rows, 2 * C + lo : 2 * C + lo + 128] = below.astype(BF16)

        def products(h, n):
            lanes = slice(n * HALF, (n + 1) * HALF)
            rows = slice(h * HALF, (h + 1) * HALF)
            return [jnp.dot(v[t, rows], u[t, :, lanes], preferred_element_type=F32) for t in range(4)]

        s[0] = jnp.where(has_left, act(halo[order, 0], coef), 0.0)
        s[COLS + 1] = jnp.where(has_right, act(halo[order, 1], coef), 0.0)
        for c in range(10):
            column(c)
        for p in range(4):
            pair(p)
        early = [products(0, 0)]
        for c in range(10, COLS):
            column(c)
        for p in range(4, 6):
            pair(p)
        early.append(products(0, 1))
        for p in range(6, PAIRS):
            pair(p)
        for n in range(2):
            lanes = slice(n * HALF, (n + 1) * HALF)
            m = [jnp.concatenate(both, axis=0) for both in zip(early[n], products(1, n))]
            finish(n, lanes, m[0] + m[1] + m[2], m[1] - m[2] - m[3])

    def moments_of(parts):
        count = sum(part.shape[0] for part in parts)
        mean = sum(jnp.sum(part, axis=0, keepdims=True) for part in parts) * (1.0 / count)
        square = sum(jnp.sum((part - mean) * (part - mean), axis=0, keepdims=True) for part in parts)
        return mean, square

    for order, fr in ((0, first_frame), (1, second_frame)):
        tiles = jnp.concatenate([st1[:, fr], st_own[fr][None]], axis=0)
        mean, square = combine(tiles, float(POS))
        coef = coefficients(mean, square, float(POS * ns), group_sum, norm1)
        edges_wait(lx, halo1, fr, order, order)
        if order == 0:
            edges_start(lx, halo1, second_frame, 1, 1)

        def finish(n, lanes, even, odd, fr=fr, order=order):
            even, odd = even + bias1[:, lanes], odd + bias1[:, lanes]
            fx[fr, :, 0, :, lanes] = even.reshape(PAIRS, ROWS, HALF).astype(BF16)
            fx[fr, :, 1, :, lanes] = odd.reshape(PAIRS, ROWS, HALF).astype(BF16)
            put_moments(st_own.at[2 + order], n * HALF, *moments_of([even, odd]))

        spatial_stage(lx, halo1, fr, order, coef, u1, finish)
        strip_gather(st_own.at[2 + order], st2.at[order], 1 + order)
        edges_start(fx, halo2, fr, order, 2 + order)

    def to_peer(order, n, lanes):
        dst = near if order == 0 else far
        fr = first_frame if order == 0 else second_frame
        return pltpu.make_async_remote_copy(
            sp.at[fr, :, :, :, lanes], dst.at[:, :, :, lanes], frame_send.at[order, n], frame_recv.at[order, n],
            device_id={"frame": peer}, device_id_type=MESH,
        )

    def to_partner(n, lanes):
        return pltpu.make_async_remote_copy(
            sp.at[second_frame, :, :, :, lanes], dd.at[:, :, :, lanes], frame_send.at[2, n], frame_recv.at[2, n],
            device_id={"frame": partner}, device_id_type=MESH,
        )

    for order, fr in ((0, first_frame), (1, second_frame)):
        gather_wait(st2.at[order], 1 + order)
        tiles = jnp.concatenate([st2[order], st_own[2 + order][None]], axis=0)
        mean, square = combine(tiles, float(POS))
        coef = coefficients(mean, square, float(POS * ns), group_sum, norm2)
        edges_wait(fx, halo2, fr, order, 2 + order)

        def finish(n, lanes, even, odd, fr=fr, order=order):
            parts = []
            for k, part in enumerate((even, odd)):
                old = lx[fr, :, k, :, lanes].astype(F32).reshape(PAIRS * ROWS, HALF)
                part = (part + bias2[:, lanes]) + old
                sp[fr, :, k, :, lanes] = part.reshape(PAIRS, ROWS, HALF).astype(BF16)
                parts.append(part)
            put_moments(st_own.at[4 + order], n * HALF, *moments_of(parts))
            if order == 0:
                pl.when(has_peer)(lambda: to_peer(0, n, lanes).start())
            if order == 1:
                to_partner(n, lanes).start()

        spatial_stage(fx, halo2, fr, order, coef, u2, finish)

    def span_first(lo, slot, k, slots):
        mean, square = combine(st_own[lo : lo + 2], float(POS))
        st_own[slot] = jnp.concatenate([mean, square], axis=0)
        strip_gather(st_own.at[slot], slots, k)

    def span_second(slot, k, slots, out_slot, out_k, out_slots):
        gather_wait(slots, k)
        mean, square = combine(jnp.concatenate([slots[...], st_own[slot][None]], axis=0), float(2 * POS))
        st_own[out_slot] = jnp.concatenate([mean, square], axis=0)
        frame_gather(st_own.at[out_slot], out_slots, out_k)

    def span_done(slot, k, slots, params):
        gather_wait(slots, k)
        mean, square = combine(jnp.concatenate([slots[...], st_own[slot][None]], axis=0), float(2 * POS * ns))
        return coefficients(mean, square, float(2 * POS * ns * nf), group_sum, params)

    span_first(4, 6, 3, st3s)
    span_second(6, 3, st3s, 7, 4, st3f)
    coef3 = span_done(7, 4, st3f, norm3)

    @pl.when(has_peer)
    def _():
        for n in range(2):
            to_peer(1, n, slice(n * HALF, (n + 1) * HALF)).start()

    def temporal_stage(fills, coef, products, tw, finish):
        for h in range(POS // HALF):
            for slot, src, kept in fills:
                for c in range(4):
                    value = act(src[2 * h + c // 2, c % 2], coef)
                    if kept is not None:
                        value = jnp.where(kept, value, 0.0)
                    lo = h * HALF + c * ROWS
                    a3[slot, lo : lo + ROWS, :] = value.astype(BF16)
            rows = slice(h * HALF, (h + 1) * HALF)
            for at in products:
                taps = jnp.concatenate([a3[at - 1, rows], a3[at, rows], a3[at + 1, rows]], axis=1)
                for n in range(2):
                    lanes = slice(n * HALF, (n + 1) * HALF)
                    finish(at, h, n, lanes, jnp.dot(taps, tw[:, lanes], preferred_element_type=F32))

    for copy in tw_loads:
        copy.wait()
    for n in range(2):
        lanes = slice(n * HALF, (n + 1) * HALF)
        copy = to_partner(n, lanes)
        copy.wait_send()
        copy.wait_recv()

    def peer_wait(order):
        @pl.when(has_peer)
        def _():
            for n in range(2):
                copy = to_peer(order, n, slice(n * HALF, (n + 1) * HALF))
                copy.wait_send()
                copy.wait_recv()

    peer_wait(0)
    blocks = {}

    def tempo_finish(at, h, n, lanes, product):
        values = product + tbias1[:, lanes]
        tm[at - 1, 2 * h : 2 * h + 2, :, :, lanes] = values.reshape(2, 2, ROWS, HALF).astype(BF16)
        if at > 1:
            blocks.setdefault((at, n), []).append(moments_of([values]))

    temporal_stage(
        [(2, sp.at[first_frame], None), (3, sp.at[second_frame], None), (4, dd, None), (1, near, has_peer)],
        coef3, (3, 2), tw1, tempo_finish,
    )
    for (at, n), parts in blocks.items():
        mean = sum(part[0] for part in parts) * (1.0 / len(parts))
        square = sum(part[1] + float(HALF) * (part[0] - mean) * (part[0] - mean) for part in parts)
        put_moments(st_own.at[6 + at], n * HALF, mean, square)
    span_first(8, 10, 5, st4s)
    tempo_copy = pltpu.make_async_remote_copy(
        tm.at[2], td, frame_send.at[3, 0], frame_recv.at[3, 0], device_id={"frame": partner}, device_id_type=MESH
    )
    tempo_copy.start()
    span_second(10, 5, st4s, 11, 6, st4f)

    peer_wait(1)
    temporal_stage([(0, far, has_peer)], coef3, (1,), tw1, tempo_finish)
    tempo_copy.wait_send()
    tempo_copy.wait_recv()

    coef4 = span_done(11, 6, st4f, norm4)
    keep = 1.0 - 1.0 / (1.0 + jnp.exp(-jnp.full((1, HALF), mix[0], F32)))
    out_copies = []

    def branch_finish(at, h, n, lanes, product):
        fr = first_frame if at == 2 else second_frame
        old = sp[fr, 2 * h : 2 * h + 2, :, :, lanes].astype(F32).reshape(HALF, HALF)
        mixed = old + keep * (product + tbias2[:, lanes])
        lx[fr, 2 * h : 2 * h + 2, :, :, lanes] = mixed.reshape(2, 2, ROWS, HALF).astype(BF16)
        if n == 1:
            part = pl.ds(2 * h, 2)
            copy = pltpu.make_async_copy(lx.at[fr, part], out_hbm.at[fr, part], out_sem.at[at - 2, h])
            copy.start()
            out_copies.append(copy)

    temporal_stage(
        [(2, tm.at[1], None), (3, tm.at[2], None), (4, td, None), (1, tm.at[0], has_peer)],
        coef4, (3, 2), tw2, branch_finish,
    )
    for copy in out_copies:
        copy.wait()


def transposition():
    i0 = lax.broadcasted_iota(jnp.int32, (HALF, HALF), 0)
    i1 = lax.broadcasted_iota(jnp.int32, (HALF, HALF), 1)
    return jnp.where(i1 == (i0 & 15) * 16 + (i0 >> 4), 1.0, 0.0).astype(BF16)


def untransposed(x, out, taken, given, taken_sem, given_sem):
    blocks = [(fr, b) for fr in range(2) for b in range(4)]
    loads = [
        pltpu.make_async_copy(x.at[fr, :, :, pl.ds(b * 16, 16), :], taken.at[n], taken_sem.at[n])
        for n, (fr, b) in enumerate(blocks)
    ]
    stores = [
        pltpu.make_async_copy(given.at[n], out.at[fr, pl.ds(b * HALF, HALF), :], given_sem.at[n])
        for n, (fr, b) in enumerate(blocks)
    ]
    for load in loads:
        load.start()
    perm = transposition()
    for n in range(8):
        loads[n].wait()
        moved = jnp.dot(perm, taken[n].reshape(HALF, C), preferred_element_type=F32)
        given[n] = moved.astype(BF16)
        stores[n].start()
    for store in stores:
        store.wait()


def body(*args):
    nf, ns = lax.axis_size("frame"), lax.axis_size("strip")
    (
        latents, norm1, conv1, bias1, norm2, conv2, bias2, norm3, time1, tbias1, norm4, time2, tbias2, mix,
    ) = args
    vmem = pl.BlockSpec(memory_space=pltpu.VMEM)
    hbm = pl.BlockSpec(memory_space=pl.ANY)
    smem = pl.BlockSpec(memory_space=pltpu.SMEM)
    tile = (8, 128)
    frame = (PAIRS, 2, ROWS, C)
    out = pl.pallas_call(
        functools.partial(kernel, nf, ns),
        out_shape=jax.ShapeDtypeStruct((2,) + frame, BF16),
        in_specs=[hbm, vmem, hbm, vmem, vmem, hbm, vmem, vmem, hbm, vmem, vmem, hbm, vmem, smem],
        out_specs=hbm,
        scratch_shapes=[
            pltpu.VMEM((2, POS, C), BF16),
            pltpu.VMEM((2,) + frame, BF16),
            pltpu.VMEM((2, 2, ROWS, C), BF16),
            pltpu.VMEM((4, 3 * C, C), BF16),
            pltpu.VMEM((4, 3 * C, C), BF16),
            pltpu.VMEM((3 * C, C), BF16),
            pltpu.VMEM((3 * C, C), BF16),
            pltpu.VMEM((COLS + 2, ROWS, C), F32),
            pltpu.VMEM((4, PAIRS * ROWS, 3 * C), BF16),
            pltpu.VMEM((2,) + frame, BF16),
            pltpu.VMEM((2, 2, ROWS, C), BF16),
            pltpu.VMEM((2,) + frame, BF16),
            pltpu.VMEM(frame, BF16),
            pltpu.VMEM(frame, BF16),
            pltpu.VMEM(frame, BF16),
            pltpu.VMEM((5, POS, C), BF16),
            pltpu.VMEM((3,) + frame, BF16),
            pltpu.VMEM(frame, BF16),
            pltpu.VMEM((HALF, HALF), BF16),
            pltpu.VMEM((12,) + tile, F32),
            pltpu.VMEM((ns - 1, 2) + tile, F32),
            pltpu.VMEM((2, ns - 1) + tile, F32),
            pltpu.VMEM((ns - 1,) + tile, F32),
            pltpu.VMEM((nf - 1,) + tile, F32),
            pltpu.VMEM((ns - 1,) + tile, F32),
            pltpu.VMEM((nf - 1,) + tile, F32),
            pltpu.SemaphoreType.DMA,
            pltpu.SemaphoreType.DMA((4, 3)),
            pltpu.SemaphoreType.DMA((4, 3)),
            pltpu.SemaphoreType.DMA((2, 3)),
            pltpu.SemaphoreType.DMA((4, 2)),
            pltpu.SemaphoreType.DMA((4, 2)),
            pltpu.SemaphoreType.DMA((7,)),
            pltpu.SemaphoreType.DMA((7,)),
            pltpu.SemaphoreType.DMA((4, 2)),
            pltpu.SemaphoreType.DMA((4, 2)),
            pltpu.SemaphoreType.DMA((2, 4)),
        ],
        compiler_params=pltpu.CompilerParams(
            collective_id=0, has_side_effects=True, vmem_limit_bytes=62 * 2**20
        ),
        cost_estimate=pl.CostEstimate(flops=20 * 10**9, bytes_accessed=17 * 2**20, transcendentals=8 * 10**6),
    )(
        latents.reshape(2, POS, C),
        norm1,
        conv1,
        bias1.reshape(1, C),
        norm2,
        conv2,
        bias2.reshape(1, C),
        norm3,
        time1,
        tbias1.reshape(1, C),
        norm4,
        time2,
        tbias2.reshape(1, C),
        mix,
    )
    rows = pl.pallas_call(
        untransposed,
        out_shape=jax.ShapeDtypeStruct((2, POS, C), BF16),
        in_specs=[hbm],
        out_specs=hbm,
        scratch_shapes=[
            pltpu.VMEM((8, PAIRS, 2, 16, C), BF16),
            pltpu.VMEM((8, HALF, C), BF16),
            pltpu.SemaphoreType.DMA((8,)),
            pltpu.SemaphoreType.DMA((8,)),
        ],
        compiler_params=pltpu.CompilerParams(vmem_limit_bytes=62 * 2**20),
        cost_estimate=pl.CostEstimate(flops=2**30, bytes_accessed=2**22, transcendentals=0),
    )(out)
    return rows.reshape(2, ROWS, COLS, C)


def solution(mesh):
    placed = (P("frame", None, "strip", None),) + (P(),) * 13
    return jax.shard_map(
        body, mesh=mesh, in_specs=placed, out_specs=P("frame", None, "strip", None), check_vma=False
    )
```
